32 devices in a mesh: ang: 4 (over y, x), strip: 8 (over z, core).
Axes of the slice: x: 2, y: 2, z: 4, core: 2. Of those that a mesh axis runs over, the one named last changes fastest.
Arguments:
- slab: bfloat16 [4, 2, 1024, 512], P('ang', None, 'strip'), may hold values from -6 to 6
- shear_taps: float32 [4, 4, 4], replicated, may hold values from -1.5 to 1.5
- band_offsets: int32 [4, 4], replicated, may hold values from -64 to 64
- probe: bfloat16 [2, 256, 256], replicated, may hold values from -6 to 6
- scan_rows: int32 [4, 32], P('ang', 'strip'), may hold values from 0 to 127
- scan_columns: int32 [4, 32], P('ang', 'strip'), may hold values from 0 to 256
- frame_counts: int32 [4, 8], P('ang', 'strip'), may hold values from 1 to 4, 16 in all within a row
- amplitudes: bfloat16 [4, 32, 256, 256], P('ang', 'strip'), may hold values from 0.19921875 to 4
Outputs:
- slab_grad: float32 [4, 2, 1024, 512], P('ang', None, 'strip')
The draws below stay inside these ranges and needn't reach their ends.
Inputs may be any that keep to these rules, and one draw needn't show every extreme that they name: `frame_counts`: for every angle the counts over the 8 strips sum to 16, and some strip has exactly 4 frames.
All inputs are finite; a program needn't handle non-finite values. No bound on the sum of `frame_counts` on one device may be relied on, other than what follows from the above.
Results may differ from the reference program's by a relative error of at most 0.013.
Values may be sent and summed in bfloat16 or wider, within the bound.
A program may use at most 64 MiB of HBM per device.

```python
import math
import jax
import jax.numpy as jnp
import numpy as np
from jax import lax

ROWS_DEV = 128
COLS = 512
FRAME = 256
TAPS = 4
MAXSHIFT = 64
MEAN = 2
CAP = 4
ANGLES = 4
SLICES = 4
STRIPS = 8
NROWS = 1024


def plant(values, key, smallest, largest):
    spot = [jax.random.randint(jax.random.fold_in(key, axis), (), 0, length) for axis, length in enumerate(values.shape)]
    main_axis = values.shape.index(max(values.shape))
    neighbour = spot[:main_axis] + [(spot[main_axis] + 1) % values.shape[main_axis]] + spot[main_axis + 1:]
    return values.at[tuple(spot)].set(smallest).at[tuple(neighbour)].set(largest)


def level_of(rng, dims, pieces, least, top_value):
    def one(axis_at, parts):
        draws = jax.random.uniform(jax.random.fold_in(jax.random.fold_in(rng, 6), axis_at), (parts,), jnp.float32, least / len(pieces), top_value / len(pieces))
        return jnp.repeat(jnp.exp(draws), dims[axis_at] // parts).reshape((-1,) + (1,) * (len(dims) - axis_at - 1))

    factor_of = one(*pieces[0])
    for cut in pieces[1:]:
        factor_of = factor_of * one(*cut)
    return factor_of


def split_up(amount, total, reach, lean):
    loads = [(1 << 20) // math.isqrt(rank ** lean) + 1 for rank in range(2, amount + 1)]
    spare, holding = total - reach - (amount - 1), [1] * (amount - 1)
    while spare > 0:
        movable = [i for i in range(amount - 1) if holding[i] < reach]
        whole, left = sum([loads[i] for i in movable]), spare
        for i in movable:
            more = min(reach - holding[i], max(1, left * loads[i] // whole), spare)
            holding[i] = holding[i] + more
            spare = spare - more
    return np.array([reach] + holding)


def ragged(key, number_of, total, limit, skew):
    if number_of == 2:
        one = jax.random.randint(key, (), max(1, total - limit), min(limit, total - 1) + 1)
        return jnp.stack([one, total - one])
    sizes = jnp.asarray(split_up(number_of, total, limit, skew), jnp.int32)
    twos = (number_of - 1) // 2
    giver, receiver = sizes[1:1 + 2 * twos:2], sizes[2:2 + 2 * twos:2]
    slack = jnp.minimum(giver - 1, limit - receiver)
    moved = jax.random.randint(jax.random.fold_in(key, 1), (twos,), 0, 1 << 20) % (slack + 1)
    sizes = sizes.at[1:1 + 2 * twos:2].set(giver - moved).at[2:2 + 2 * twos:2].set(receiver + moved)
    return sizes[jax.random.permutation(jax.random.fold_in(key, 2), number_of)]


def centred(key, extent, scale, reach, split=(), held_as=jnp.bfloat16):
    level = level_of(key, extent, split, -0.22, 0.18) if split else 1.0
    result = jax.random.normal(key, extent, jnp.float32) * scale * level
    return jnp.minimum(jnp.maximum(result, -reach), reach).astype(held_as)


def setup_inputs(seed: int = 0) -> dict:
    keys = jax.random.split(jax.random.key(seed), 9)
    return {
        "slab": centred(keys[0], (SLICES, 2, NROWS, COLS), 1.0, 6.0, ((0, 4), (2, 8))),
        "shear_taps": centred(keys[1], (TAPS, ANGLES, SLICES), (SLICES * TAPS) ** -0.5, 1.5, (), jnp.float32),
        "band_offsets": plant(jax.random.randint(keys[2], (ANGLES, SLICES), 0 - MAXSHIFT, MAXSHIFT + 1), jax.random.fold_in(keys[2], 1), 0 - MAXSHIFT, MAXSHIFT).astype(jnp.int32),
        "probe": centred(keys[3], (2, FRAME, FRAME), 1.0, 6.0),
        "scan_rows": plant(jax.random.randint(keys[4], (ANGLES, STRIPS * CAP), 0, ROWS_DEV), jax.random.fold_in(keys[4], 1), 0, ROWS_DEV - 1).astype(jnp.int32),
        "scan_columns": plant(jax.random.randint(keys[5], (ANGLES, STRIPS * CAP), 0, COLS - FRAME + 1), jax.random.fold_in(keys[5], 1), 0, COLS - FRAME).astype(jnp.int32),
        "frame_counts": jax.vmap(lambda own: ragged(own, STRIPS, MEAN * STRIPS, CAP, 2))(jax.random.split(keys[6], ANGLES)).reshape((ANGLES, STRIPS)).astype(jnp.int32),
        "amplitudes": jnp.clip(jnp.exp(math.log(4.0) - 2.9996462 * jax.random.uniform(keys[7], (ANGLES, STRIPS * CAP, FRAME, FRAME), jnp.float32) ** level_of(keys[7], (ANGLES, STRIPS * CAP, FRAME, FRAME), ((0, 4), (1, 8)), -0.2, 0.2)), 0.19921875, 4.0).astype(jnp.bfloat16),
    }


def dft_tables(length):
    index = jnp.arange(length, dtype=jnp.int32)
    product = index[:, None] * index[None, :] % length
    phase = product.astype(jnp.float32) * (2.0 * math.pi / length)
    scale = 1.0 / math.sqrt(length)
    return ((jnp.cos(phase) * scale).astype(jnp.bfloat16), (jnp.sin(phase) * scale).astype(jnp.bfloat16))

def product_left(matrix, batch):
    return jnp.einsum('ij,bjk->bik', matrix.astype(jnp.float32), batch.astype(jnp.float32), precision=lax.Precision.HIGHEST)

def product_right(batch, matrix):
    return jnp.einsum('bij,jk->bik', batch.astype(jnp.float32), matrix.astype(jnp.float32), precision=lax.Precision.HIGHEST)

def frame_gradient(patch, probe, amplitudes):
    length = probe.shape[1]
    cosine, sine = dft_tables(length)
    forward_left = jnp.concatenate([jnp.concatenate([cosine, sine], 1), jnp.concatenate([-sine, cosine], 1)], 0)
    inverse_left = jnp.concatenate([jnp.concatenate([cosine, -sine], 1), jnp.concatenate([sine, cosine], 1)], 0)
    right = jnp.concatenate([cosine, sine], 1)
    probe_real = probe[0].astype(jnp.float32)
    probe_imag = probe[1].astype(jnp.float32)
    patch_real = patch[:, 0]
    patch_imag = patch[:, 1]
    exit_wave = jnp.concatenate([probe_real * patch_real - probe_imag * patch_imag, probe_real * patch_imag + probe_imag * patch_real], axis=1).astype(jnp.bfloat16)
    half = product_left(forward_left, exit_wave).astype(jnp.bfloat16)
    far = product_right(half, right)
    far_real = far[:, :length, :length] + far[:, length:, length:]
    far_imag = far[:, length:, :length] - far[:, :length, length:]
    factor = 1.0 - amplitudes.astype(jnp.float32) / jnp.sqrt(far_real * far_real + far_imag * far_imag + 1.0)
    residual = jnp.concatenate([far_real * factor, far_imag * factor], axis=1).astype(jnp.bfloat16)
    back_half = product_left(inverse_left, residual).astype(jnp.bfloat16)
    back = product_right(back_half, right)
    back_real = back[:, :length, :length] - back[:, length:, length:]
    back_imag = back[:, length:, :length] + back[:, :length, length:]
    grad_real = probe_real * back_real + probe_imag * back_imag
    grad_imag = probe_real * back_imag - probe_imag * back_real
    return jnp.stack([grad_real, grad_imag], axis=1)

def add_taps(total, source, shear_taps, band_offsets, angle, depth, sign, width):
    margin = MAXSHIFT + TAPS
    for tap in range(TAPS):
        start = (margin + sign * (band_offsets[angle, depth] + tap)).astype(jnp.int32)
        piece = lax.dynamic_slice_in_dim(source, start, width, axis=2)
        total = total + shear_taps[tap, angle, depth] * piece
    return total

def reference(slab, shear_taps, band_offsets, probe, scan_rows, scan_columns, frame_counts, amplitudes):
    margin = MAXSHIFT + TAPS
    padded_slab = jnp.pad(slab.astype(jnp.float32), ((0, 0), (0, 0), (0, 0), (margin, margin)))

    def project_angle(angle):

        def add_slice(depth, total):
            return add_taps(total, padded_slab[depth], shear_taps, band_offsets, angle, depth, 1, COLS)
        return lax.fori_loop(0, SLICES, add_slice, jnp.zeros((2, NROWS, COLS), jnp.float32))
    projection = lax.map(project_angle, jnp.arange(ANGLES, dtype=jnp.int32))
    rim = FRAME // 2
    extended = jnp.pad(projection, ((0, 0), (0, 0), (rim, rim), (0, 0)))
    anchor = jnp.zeros((), jnp.int32)

    def angle_image(angle):
        picture = extended[angle]

        def strip_step(strip, acc):
            first = (strip * CAP).astype(jnp.int32)
            row_starts = lax.dynamic_slice_in_dim(scan_rows[angle], first, CAP) + (strip * ROWS_DEV).astype(jnp.int32)
            column_starts = lax.dynamic_slice_in_dim(scan_columns[angle], first, CAP)
            measured = lax.dynamic_slice_in_dim(amplitudes[angle], first, CAP)
            live = (jnp.arange(CAP, dtype=jnp.int32) < frame_counts[angle, strip]).astype(jnp.float32)

            def cut_patch(row, column):
                return lax.dynamic_slice(picture, (anchor, row, column), (2, FRAME, FRAME))
            patches = jax.vmap(cut_patch)(row_starts, column_starts)
            gradients = frame_gradient(patches, probe, measured) * live[:, None, None, None]

            def place(which, inner):
                corner = (anchor, row_starts[which], column_starts[which])
                current = lax.dynamic_slice(inner, corner, (2, FRAME, FRAME))
                return lax.dynamic_update_slice(inner, current + gradients[which], corner)
            return lax.fori_loop(0, CAP, place, acc)
        placed = lax.fori_loop(0, STRIPS, strip_step, jnp.zeros((2, NROWS + FRAME, COLS), jnp.float32))
        return placed[:, rim:rim + NROWS].astype(jnp.bfloat16)
    image = lax.map(angle_image, jnp.arange(ANGLES, dtype=jnp.int32))
    padded_image = jnp.pad(image.astype(jnp.float32), ((0, 0), (0, 0), (0, 0), (margin, margin)))

    def back_slice(depth):

        def add_angle(angle, total):
            return add_taps(total, padded_image[angle], shear_taps, band_offsets, angle, depth, -1, COLS)
        return lax.fori_loop(0, ANGLES, add_angle, jnp.zeros((2, NROWS, COLS), jnp.float32))
    return lax.map(back_slice, jnp.arange(SLICES, dtype=jnp.int32))
```

```python
import functools
import math

import jax
import jax.numpy as jnp
import ml_dtypes
import numpy as np
from jax import lax
from jax.experimental import pallas as pl
from jax.experimental.pallas import tpu as pltpu
from jax.sharding import PartitionSpec as P

MESH = pl.DeviceIdType.MESH
BF = jnp.bfloat16
F32 = jnp.float32


def dft_blocks(length):
    index = np.arange(length)
    phase = (np.outer(index, index) % length).astype(np.float32) * np.float32(2.0 * math.pi / length)
    scale = np.float32(1.0 / math.sqrt(length))
    cosine = (np.cos(phase) * scale).astype(ml_dtypes.bfloat16)
    sine = (np.sin(phase) * scale).astype(ml_dtypes.bfloat16)
    first = np.block([[cosine, sine], [-sine, cosine]])
    return first, np.ascontiguousarray(first.T)


def kernel(
    n, strips, chunks, slab, taps, offsets, probe, scan_rows, scan_columns, counts, amplitudes,
    wf, wg, out, ga, gb, bands_f, bands_b, ext, acc, edges, edge_in, img,
    a_send, a_recv, h_send, h_recv, e_send, e_recv, b_send, b_recv,
):
    rows, width = slab.shape[2], slab.shape[3]
    length = probe.shape[1]
    slots = amplitudes.shape[1]
    tap_count = taps.shape[0]
    size = rows // chunks
    ang = lax.axis_index("ang")
    strip = lax.axis_index("strip")
    has_up = strip > 0
    has_down = strip < strips - 1
    square = n == 4
    if square:
        ax, ay = ang % 2, ang // 2
        near_x, near_y = ay * 2 + (1 - ax), (1 - ay) * 2 + ax
        order = [ang, near_x, near_y, (1 - ay) * 2 + (1 - ax)]
        peers = [near_x, near_y]
    else:
        order = [(ang + n - k) % n for k in range(n)]
        peers = [(ang + k) % n for k in range(1, n)]

    barrier = pltpu.get_barrier_semaphore()
    for peer in peers:
        pl.semaphore_signal(barrier, inc=1, device_id=(peer, strip), device_id_type=MESH)

    @pl.when(has_up)
    def _():
        pl.semaphore_signal(barrier, inc=1, device_id=(ang, strip - 1), device_id_type=MESH)

    @pl.when(has_down)
    def _():
        pl.semaphore_signal(barrier, inc=1, device_id=(ang, strip + 1), device_id_type=MESH)

    sides = (strip + strips - 1) // strips + 1 - (strip + 1) // strips
    pl.semaphore_wait(barrier, len(peers) + sides)

    def part(c):
        return pl.ds(c * size, size)

    def copy(src, dst, send, recv, device):
        return pltpu.make_async_remote_copy(
            src_ref=src, dst_ref=dst, send_sem=send, recv_sem=recv,
            device_id=device, device_id_type=MESH,
        )

    def gather_copy(own, g, send, recv, c, kind):
        if square and kind == 2:
            source, peer = (1, near_y) if c % 2 == 0 else (2, near_x)
            source = g.at[source, :, part(c), :]
        else:
            source, peer = own.at[:, part(c), :], peers[kind]
        return copy(
            source, g.at[kind + 1, :, part(c), :], send.at[kind, c], recv.at[kind, c], (peer, strip)
        )

    def gather_start(own, g, send, recv, c):
        for kind in range(len(peers)):
            gather_copy(own, g, send, recv, c, kind).start()

    def gather_forward(own, g, send, recv, c):
        if square:
            gather_copy(own, g, send, recv, c, c % 2).wait_recv()
            gather_copy(own, g, send, recv, c, 2).start()

    def gather_wait(own, g, send, recv, c):
        for kind in range(n - 1):
            if not (square and kind == c % 2):
                gather_copy(own, g, send, recv, c, kind).wait_recv()

    def gather_sent(own, g, send, recv):
        for c in range(chunks):
            for kind in range(n - 1):
                gather_copy(own, g, send, recv, c, kind).wait_send()

    def strip_copy(src, dst, send, recv, c, way):
        return copy(
            src.at[:, part(c), :], dst.at[way, :, part(c), :], send.at[way, c], recv.at[way, c],
            (ang, strip - 1 if way == 0 else strip + 1),
        )

    def halo_copy(c, way):
        target = 2 * rows if way == 0 else 0
        return copy(
            ext.at[:, pl.ds(rows + c * size, size), :],
            ext.at[:, pl.ds(target + c * size, size), :],
            h_send.at[way, c], h_recv.at[way, c], (ang, strip - 1 if way == 0 else strip + 1),
        )

    def band(k, sign, store):
        if sign > 0:
            angle, depth = ang, order[k]
        else:
            angle, depth = order[k], ang
        offset = offsets[angle, depth]
        weights = [taps[t, angle, depth] for t in range(tap_count)]
        step = 64

        @pl.loop(0, width // step)
        def _(i):
            shape = (step, width)
            source = lax.broadcasted_iota(jnp.int32, shape, 0) + i * step
            target = lax.broadcasted_iota(jnp.int32, shape, 1)
            tap = (source - target) * sign - offset
            value = jnp.zeros(shape, F32)
            for t in range(tap_count):
                value = jnp.where(tap == t, weights[t], value)
            store[k, pl.ds(pl.multiple_of(i * step, step), step), :] = value.astype(BF)

    def apply(own, g, bands, c):
        total = None
        for k in range(n):
            block = own[:, part(c), :] if k == 0 else g[k, :, part(c), :]
            term = jnp.dot(
                block.reshape(2 * size, width), bands[k], preferred_element_type=F32
            )
            total = term if total is None else total + term
        return total.reshape(2, size, width)

    first = slab.at[0]
    for c in range(chunks):
        gather_start(first, ga, a_send, a_recv, c)
    for k in range(n):
        band(k, 1, bands_f)
    for c in range(chunks):
        gather_forward(first, ga, a_send, a_recv, c)
    for k in range(n):
        band(k, -1, bands_b)
    acc[...] = jnp.zeros_like(acc)
    for c in range(chunks):
        gather_wait(first, ga, a_send, a_recv, c)
        piece = apply(first, ga, bands_f, c)
        ext[:, pl.ds(rows + c * size, size), :] = piece.astype(BF)

        @pl.when(has_up)
        def _():
            halo_copy(c, 0).start()

        @pl.when(has_down)
        def _():
            halo_copy(c, 1).start()

    @pl.when(has_up)
    def _():
        for c in range(chunks):
            halo_copy(c, 1).wait_recv()

    @pl.when(jnp.logical_not(has_up))
    def _():
        ext[:, :rows, :] = jnp.zeros((2, rows, width), BF)

    @pl.when(has_down)
    def _():
        for c in range(chunks):
            halo_copy(c, 0).wait_recv()

    @pl.when(jnp.logical_not(has_down))
    def _():
        ext[:, 2 * rows :, :] = jnp.zeros((2, rows, width), BF)

    def picks(shape, first, second, shift, live=None):
        hit = (
            lax.broadcasted_iota(jnp.int32, shape, second)
            - lax.broadcasted_iota(jnp.int32, shape, first)
        ) == shift
        if live is not None:
            hit = jnp.logical_and(hit, live)
        return jnp.where(hit, 1.0, 0.0).astype(BF)

    tall = length + rows

    def frame(f, carry):
        row = scan_rows[0, f]
        column = scan_columns[0, f]
        probe_real = probe[0].astype(F32)
        probe_imag = probe[1].astype(F32)
        cut = jnp.dot(
            ext[...].reshape(2 * tall, width), picks((width, length), 1, 0, column),
            preferred_element_type=F32,
        ).astype(BF)
        patch = jnp.dot(
            picks((length, tall), 0, 1, row),
            jnp.concatenate([cut[:tall], cut[tall:]], axis=1),
            preferred_element_type=F32,
        )
        patch_real, patch_imag = patch[:, :length], patch[:, length:]
        wave = jnp.concatenate(
            [
                (probe_real * patch_real - probe_imag * patch_imag).astype(BF),
                (probe_real * patch_imag + probe_imag * patch_real).astype(BF),
            ],
            axis=0,
        )
        half = jnp.dot(wf[...], wave, preferred_element_type=F32).astype(BF)
        half = jnp.concatenate([half[:length], half[length:]], axis=1)
        far = jnp.dot(half, wg[...], preferred_element_type=F32)
        far_real, far_imag = far[:, :length], far[:, length:]
        factor = 1.0 - amplitudes[0, f].astype(F32) * lax.rsqrt(
            far_real * far_real + far_imag * far_imag + 1.0
        )
        residual = jnp.concatenate(
            [(far_real * factor).astype(BF), (far_imag * factor).astype(BF)], axis=0
        )
        back_half = jnp.dot(wg[...], residual, preferred_element_type=F32).astype(BF)
        back_half = jnp.concatenate([back_half[:length], back_half[length:]], axis=1)
        back = jnp.dot(back_half, wf[...], preferred_element_type=F32)
        back_real, back_imag = back[:, :length], back[:, length:]
        grad = jnp.concatenate(
            [
                (probe_real * back_real + probe_imag * back_imag).astype(BF),
                (probe_real * back_imag - probe_imag * back_real).astype(BF),
            ],
            axis=0,
        )
        placed = jnp.dot(
            grad, picks((length, width), 0, 1, column), preferred_element_type=F32
        ).astype(BF)
        shape = (tall, length)
        live = lax.broadcasted_iota(jnp.int32, shape, 0) * 0 + f < counts[0, 0]
        placed = jnp.dot(
            picks(shape, 1, 0, row, live),
            jnp.concatenate([placed[:length], placed[length:]], axis=1),
            preferred_element_type=F32,
        )
        acc[0] += placed[:, :width]
        acc[1] += placed[:, width:]
        return carry

    lax.fori_loop(0, slots, frame, 0)

    for c in range(chunks):
        for way, base in ((0, 0), (1, 2 * rows)):
            edges[way, :, part(c), :] = acc[:, pl.ds(base + c * size, size), :].astype(BF)

        @pl.when(has_up)
        def _():
            strip_copy(edges.at[0], edge_in, e_send, e_recv, c, 0).start()

        @pl.when(has_down)
        def _():
            strip_copy(edges.at[1], edge_in, e_send, e_recv, c, 1).start()

    for c in range(chunks):
        middle = pl.ds(rows + c * size, size)

        @pl.when(has_up)
        def _():
            strip_copy(edges.at[1], edge_in, e_send, e_recv, c, 1).wait_recv()
            acc[:, middle, :] += edge_in[1, :, part(c), :].astype(F32)

        @pl.when(has_down)
        def _():
            strip_copy(edges.at[0], edge_in, e_send, e_recv, c, 0).wait_recv()
            acc[:, middle, :] += edge_in[0, :, part(c), :].astype(F32)

        img[:, part(c), :] = acc[:, middle, :].astype(BF)
        gather_start(img, gb, b_send, b_recv, c)
    for c in range(chunks):
        gather_forward(img, gb, b_send, b_recv, c)
    for c in range(chunks):
        gather_wait(img, gb, b_send, b_recv, c)
        out[0, :, part(c), :] = apply(img, gb, bands_b, c)

    gather_sent(first, ga, a_send, a_recv)
    gather_sent(img, gb, b_send, b_recv)
    for way, here in ((0, has_up), (1, has_down)):

        @pl.when(here)
        def _(way=way):
            for c in range(chunks):
                halo_copy(c, way).wait_send()
                strip_copy(edges.at[way], edge_in, e_send, e_recv, c, way).wait_send()


def per_device(
    n, strips, slab, shear_taps, band_offsets, probe, scan_rows, scan_columns, frame_counts, amplitudes
):
    rows, width = slab.shape[2], slab.shape[3]
    length = probe.shape[1]
    chunks = 2
    wf, wg = dft_blocks(length)
    vmem = pl.BlockSpec(memory_space=pltpu.VMEM)
    smem = pl.BlockSpec(memory_space=pltpu.SMEM)
    dma = pltpu.SemaphoreType.DMA
    field = (2, rows, width)
    return pl.pallas_call(
        functools.partial(kernel, n, strips, chunks),
        out_shape=jax.ShapeDtypeStruct((1,) + field, F32),
        in_specs=[vmem, smem, smem, vmem, smem, smem, smem, vmem, vmem, vmem],
        out_specs=vmem,
        scratch_shapes=[
            pltpu.VMEM((n,) + field, BF),
            pltpu.VMEM((n,) + field, BF),
            pltpu.VMEM((n, width, width), BF),
            pltpu.VMEM((n, width, width), BF),
            pltpu.VMEM((2, length + rows, width), BF),
            pltpu.VMEM((2, length + rows, width), F32),
            pltpu.VMEM((2,) + field, BF),
            pltpu.VMEM((2,) + field, BF),
            pltpu.VMEM(field, BF),
            dma((n - 1, chunks)), dma((n - 1, chunks)),
            dma((2, chunks)), dma((2, chunks)),
            dma((2, chunks)), dma((2, chunks)),
            dma((n - 1, chunks)), dma((n - 1, chunks)),
        ],
        compiler_params=pltpu.CompilerParams(
            collective_id=0, has_side_effects=True, vmem_limit_bytes=48 << 20
        ),
    )(
        slab, shear_taps, band_offsets, probe, scan_rows, scan_columns, frame_counts, amplitudes,
        jnp.asarray(wf), jnp.asarray(wg),
    )


def solution(mesh):
    return jax.shard_map(
        functools.partial(per_device, mesh.shape["ang"], mesh.shape["strip"]),
        mesh=mesh,
        in_specs=(
            P("ang", None, "strip", None),
            P(),
            P(),
            P(),
            P("ang", "strip"),
            P("ang", "strip"),
            P("ang", "strip"),
            P("ang", "strip", None, None),
        ),
        out_specs=P("ang", None, "strip", None),
        check_vma=False,
    )
```

```python
import functools
import math

import jax
import jax.numpy as jnp
import ml_dtypes
import numpy as np
from jax import lax
from jax.experimental import pallas as pl
from jax.experimental.pallas import tpu as pltpu
from jax.sharding import PartitionSpec as P

MESH = pl.DeviceIdType.MESH
BF = jnp.bfloat16
F32 = jnp.float32


def dft_blocks(length):
    index = np.arange(length)
    phase = (np.outer(index, index) % length).astype(np.float32) * np.float32(2.0 * math.pi / length)
    scale = np.float32(1.0 / math.sqrt(length))
    cosine = (np.cos(phase) * scale).astype(ml_dtypes.bfloat16)
    sine = (np.sin(phase) * scale).astype(ml_dtypes.bfloat16)
    return np.block([[cosine, sine], [-sine, cosine]])


def kernel(
    n, strips, chunks, *refs,
):
    inputs, out, held, rest = refs[:9], refs[9], refs[10:19], refs[19:]
    slab, taps, offsets, probe, scan_rows, scan_columns, counts, amplitudes, wf = held
    (
        load, wg, ga, gb,
        bands_f, bands_b, ext, acc, edges, edge_in, img,
        a_send, a_recv, h_send, h_recv, e_send, e_recv, b_send, b_recv,
    ) = rest
    loads = [
        pltpu.make_async_copy(inputs[i], held[i], load.at[i]) for i in range(len(inputs))
    ]
    for each in loads:
        each.start()
    rows, width = slab.shape[2], slab.shape[3]
    length = probe.shape[1]
    slots = amplitudes.shape[1]
    tap_count = taps.shape[0]
    size = rows // chunks
    ang = lax.axis_index("ang")
    strip = lax.axis_index("strip")
    has_up = strip > 0
    has_down = strip < strips - 1
    square = n == 4
    if square:
        ax, ay = ang % 2, ang // 2
        near_x, near_y = ay * 2 + (1 - ax), (1 - ay) * 2 + ax
        order = [ang, near_x, near_y, (1 - ay) * 2 + (1 - ax)]
        peers = [near_x, near_y]
    else:
        order = [(ang + n - k) % n for k in range(n)]
        peers = [(ang + k) % n for k in range(1, n)]

    barrier = pltpu.get_barrier_semaphore()
    for peer in peers:
        pl.semaphore_signal(barrier, inc=1, device_id=(peer, strip), device_id_type=MESH)

    @pl.when(has_up)
    def _():
        pl.semaphore_signal(barrier, inc=1, device_id=(ang, strip - 1), device_id_type=MESH)

    @pl.when(has_down)
    def _():
        pl.semaphore_signal(barrier, inc=1, device_id=(ang, strip + 1), device_id_type=MESH)

    sides = (strip + strips - 1) // strips + 1 - (strip + 1) // strips
    pl.semaphore_wait(barrier, len(peers) + sides)

    def part(c):
        return pl.ds(c * size, size)

    def copy(src, dst, send, recv, device):
        return pltpu.make_async_remote_copy(
            src_ref=src, dst_ref=dst, send_sem=send, recv_sem=recv,
            device_id=device, device_id_type=MESH,
        )

    def gather_copy(own, g, send, recv, c, kind):
        if square and kind == 2:
            source, peer = (1, near_y) if c % 2 == 0 else (2, near_x)
            source = g.at[source, :, part(c), :]
        else:
            source, peer = own.at[:, part(c), :], peers[kind]
        return copy(
            source, g.at[kind + 1, :, part(c), :], send.at[kind, c], recv.at[kind, c], (peer, strip)
        )

    def gather_start(own, g, send, recv, c):
        for kind in range(len(peers)):
            gather_copy(own, g, send, recv, c, kind).start()

    def gather_forward(own, g, send, recv, c):
        if square:
            gather_copy(own, g, send, recv, c, c % 2).wait_recv()
            gather_copy(own, g, send, recv, c, 2).start()

    def gather_wait(own, g, send, recv, c):
        for kind in range(n - 1):
            if not (square and kind == c % 2):
                gather_copy(own, g, send, recv, c, kind).wait_recv()

    def gather_sent(own, g, send, recv):
        for c in range(chunks):
            for kind in range(n - 1):
                gather_copy(own, g, send, recv, c, kind).wait_send()

    def strip_copy(src, dst, send, recv, c, way):
        return copy(
            src.at[:, part(c), :], dst.at[way, :, part(c), :], send.at[way, c], recv.at[way, c],
            (ang, strip - 1 if way == 0 else strip + 1),
        )

    def halo_copy(c, way):
        target = 2 * rows if way == 0 else 0
        return copy(
            ext.at[:, pl.ds(rows + c * size, size), :],
            ext.at[:, pl.ds(target + c * size, size), :],
            h_send.at[way, c], h_recv.at[way, c], (ang, strip - 1 if way == 0 else strip + 1),
        )

    def band(k, sign, store):
        if sign > 0:
            angle, depth = ang, order[k]
        else:
            angle, depth = order[k], ang
        offset = offsets[angle, depth]
        weights = [taps[t, angle, depth] for t in range(tap_count)]
        step = 64

        @pl.loop(0, width // step)
        def _(i):
            shape = (step, width)
            source = lax.broadcasted_iota(jnp.int32, shape, 0) + i * step
            target = lax.broadcasted_iota(jnp.int32, shape, 1)
            tap = (source - target) * sign - offset
            value = jnp.zeros(shape, F32)
            for t in range(tap_count):
                value = jnp.where(tap == t, weights[t], value)
            store[k, pl.ds(pl.multiple_of(i * step, step), step), :] = value.astype(BF)

    def apply(own, g, bands, c):
        total = None
        for k in range(n):
            block = own[:, part(c), :] if k == 0 else g[k, :, part(c), :]
            term = jnp.dot(
                block.reshape(2 * size, width), bands[k], preferred_element_type=F32
            )
            total = term if total is None else total + term
        return total.reshape(2, size, width)

    first = slab.at[0]
    loads[0].wait()
    for c in range(chunks):
        gather_start(first, ga, a_send, a_recv, c)
    for i in (1, 2):
        loads[i].wait()
    for k in range(n):
        band(k, 1, bands_f)
    for c in range(chunks):
        gather_forward(first, ga, a_send, a_recv, c)
    for k in range(n):
        band(k, -1, bands_b)
    acc[...] = jnp.zeros_like(acc)
    for each in loads[3:]:
        each.wait()
    wg[:length, :] = jnp.concatenate([wf[:length, :length], wf[length:, :length]], axis=1)
    wg[length:, :] = jnp.concatenate(
        [wf[:length, length:], wf[:length, :length]], axis=1
    )
    for c in range(chunks):
        gather_wait(first, ga, a_send, a_recv, c)
        piece = apply(first, ga, bands_f, c)
        ext[:, pl.ds(rows + c * size, size), :] = piece.astype(BF)

        @pl.when(has_up)
        def _():
            halo_copy(c, 0).start()

        @pl.when(has_down)
        def _():
            halo_copy(c, 1).start()

    @pl.when(has_up)
    def _():
        for c in range(chunks):
            halo_copy(c, 1).wait_recv()

    @pl.when(jnp.logical_not(has_up))
    def _():
        ext[:, :rows, :] = jnp.zeros((2, rows, width), BF)

    @pl.when(has_down)
    def _():
        for c in range(chunks):
            halo_copy(c, 0).wait_recv()

    @pl.when(jnp.logical_not(has_down))
    def _():
        ext[:, 2 * rows :, :] = jnp.zeros((2, rows, width), BF)

    def picks(shape, first, second, shift, live=None):
        hit = (
            lax.broadcasted_iota(jnp.int32, shape, second)
            - lax.broadcasted_iota(jnp.int32, shape, first)
        ) == shift
        if live is not None:
            hit = jnp.logical_and(hit, live)
        return jnp.where(hit, 1.0, 0.0).astype(BF)

    tall = length + rows

    def frame(f, carry):
        row = scan_rows[0, f]
        column = scan_columns[0, f]
        probe_real = probe[0].astype(F32)
        probe_imag = probe[1].astype(F32)
        cut = jnp.dot(
            ext[...].reshape(2 * tall, width), picks((width, length), 1, 0, column),
            preferred_element_type=F32,
        ).astype(BF)
        patch = jnp.dot(
            picks((length, tall), 0, 1, row),
            jnp.concatenate([cut[:tall], cut[tall:]], axis=1),
            preferred_element_type=F32,
        )
        patch_real, patch_imag = patch[:, :length], patch[:, length:]
        wave = jnp.concatenate(
            [
                (probe_real * patch_real - probe_imag * patch_imag).astype(BF),
                (probe_real * patch_imag + probe_imag * patch_real).astype(BF),
            ],
            axis=0,
        )
        half = jnp.dot(wf[...], wave, preferred_element_type=F32).astype(BF)
        half = jnp.concatenate([half[:length], half[length:]], axis=1)
        far = jnp.dot(half, wg[...], preferred_element_type=F32)
        far_real, far_imag = far[:, :length], far[:, length:]
        factor = 1.0 - amplitudes[0, f].astype(F32) * lax.rsqrt(
            far_real * far_real + far_imag * far_imag + 1.0
        )
        residual = jnp.concatenate(
            [(far_real * factor).astype(BF), (far_imag * factor).astype(BF)], axis=0
        )
        back_half = jnp.dot(wg[...], residual, preferred_element_type=F32).astype(BF)
        back_half = jnp.concatenate([back_half[:length], back_half[length:]], axis=1)
        back = jnp.dot(back_half, wf[...], preferred_element_type=F32)
        back_real, back_imag = back[:, :length], back[:, length:]
        grad = jnp.concatenate(
            [
                (probe_real * back_real + probe_imag * back_imag).astype(BF),
                (probe_real * back_imag - probe_imag * back_real).astype(BF),
            ],
            axis=0,
        )
        placed = jnp.dot(
            grad, picks((length, width), 0, 1, column), preferred_element_type=F32
        ).astype(BF)
        shape = (tall, length)
        live = lax.broadcasted_iota(jnp.int32, shape, 0) * 0 + f < counts[0, 0]
        placed = jnp.dot(
            picks(shape, 1, 0, row, live),
            jnp.concatenate([placed[:length], placed[length:]], axis=1),
            preferred_element_type=F32,
        )
        acc[0] += placed[:, :width]
        acc[1] += placed[:, width:]
        return carry

    lax.fori_loop(0, slots, frame, 0, unroll=True)

    for c in range(chunks):
        for way, base in ((0, 0), (1, 2 * rows)):
            edges[way, :, part(c), :] = acc[:, pl.ds(base + c * size, size), :].astype(BF)

        @pl.when(has_up)
        def _():
            strip_copy(edges.at[0], edge_in, e_send, e_recv, c, 0).start()

        @pl.when(has_down)
        def _():
            strip_copy(edges.at[1], edge_in, e_send, e_recv, c, 1).start()

    for c in range(chunks):
        middle = pl.ds(rows + c * size, size)

        @pl.when(has_up)
        def _():
            strip_copy(edges.at[1], edge_in, e_send, e_recv, c, 1).wait_recv()
            acc[:, middle, :] += edge_in[1, :, part(c), :].astype(F32)

        @pl.when(has_down)
        def _():
            strip_copy(edges.at[0], edge_in, e_send, e_recv, c, 0).wait_recv()
            acc[:, middle, :] += edge_in[0, :, part(c), :].astype(F32)

        img[:, part(c), :] = acc[:, middle, :].astype(BF)
        gather_start(img, gb, b_send, b_recv, c)
    for c in range(chunks):
        gather_forward(img, gb, b_send, b_recv, c)
    for c in range(chunks):
        gather_wait(img, gb, b_send, b_recv, c)
        out[0, :, part(c), :] = apply(img, gb, bands_b, c)

    gather_sent(first, ga, a_send, a_recv)
    gather_sent(img, gb, b_send, b_recv)
    for way, here in ((0, has_up), (1, has_down)):

        @pl.when(here)
        def _(way=way):
            for c in range(chunks):
                halo_copy(c, way).wait_send()
                strip_copy(edges.at[way], edge_in, e_send, e_recv, c, way).wait_send()


def per_device(
    n, strips, slab, shear_taps, band_offsets, probe, scan_rows, scan_columns, frame_counts, amplitudes
):
    rows, width = slab.shape[2], slab.shape[3]
    length = probe.shape[1]
    chunks = 2
    wf = dft_blocks(length)
    small = (1, 2, 4, 5, 6)
    operands = (
        slab, shear_taps, band_offsets, probe, scan_rows, scan_columns, frame_counts, amplitudes,
        jnp.asarray(wf),
    )
    dma = pltpu.SemaphoreType.DMA
    field = (2, rows, width)
    return pl.pallas_call(
        functools.partial(kernel, n, strips, chunks),
        out_shape=jax.ShapeDtypeStruct((1,) + field, F32),
        in_specs=[pl.BlockSpec(memory_space=pltpu.HBM)] * len(operands),
        out_specs=pl.BlockSpec(memory_space=pltpu.VMEM),
        scratch_shapes=[
            (pltpu.SMEM if i in small else pltpu.VMEM)(x.shape, x.dtype)
            for i, x in enumerate(operands)
        ]
        + [
            dma((len(operands),)),
            pltpu.VMEM(wf.shape, BF),
            pltpu.VMEM((n,) + field, BF),
            pltpu.VMEM((n,) + field, BF),
            pltpu.VMEM((n, width, width), BF),
            pltpu.VMEM((n, width, width), BF),
            pltpu.VMEM((2, length + rows, width), BF),
            pltpu.VMEM((2, length + rows, width), F32),
            pltpu.VMEM((2,) + field, BF),
            pltpu.VMEM((2,) + field, BF),
            pltpu.VMEM(field, BF),
            dma((n - 1, chunks)), dma((n - 1, chunks)),
            dma((2, chunks)), dma((2, chunks)),
            dma((2, chunks)), dma((2, chunks)),
            dma((n - 1, chunks)), dma((n - 1, chunks)),
        ],
        compiler_params=pltpu.CompilerParams(
            collective_id=0, has_side_effects=True, vmem_limit_bytes=62 << 20
        ),
    )(*operands)


def solution(mesh):
    return jax.shard_map(
        functools.partial(per_device, mesh.shape["ang"], mesh.shape["strip"]),
        mesh=mesh,
        in_specs=(
            P("ang", None, "strip", None),
            P(),
            P(),
            P(),
            P("ang", "strip"),
            P("ang", "strip"),
            P("ang", "strip"),
            P("ang", "strip", None, None),
        ),
        out_specs=P("ang", None, "strip", None),
        check_vma=False,
    )
```

```python
import functools
import math

import jax
import jax.numpy as jnp
import ml_dtypes
import numpy as np
from jax import lax
from jax.experimental import pallas as pl
from jax.experimental.pallas import tpu as pltpu
from jax.sharding import PartitionSpec as P

MESH = pl.DeviceIdType.MESH
BF = jnp.bfloat16
F32 = jnp.float32


def dft_blocks(length):
    index = np.arange(length)
    phase = (np.outer(index, index) % length).astype(np.float32) * np.float32(2.0 * math.pi / length)
    scale = np.float32(1.0 / math.sqrt(length))
    cosine = (np.cos(phase) * scale).astype(ml_dtypes.bfloat16)
    sine = (np.sin(phase) * scale).astype(ml_dtypes.bfloat16)
    return np.block([[cosine, sine], [-sine, cosine]])


def kernel(
    n, strips, chunks, *refs,
):
    inputs, out, held, rest = refs[:9], refs[9], refs[10:19], refs[19:]
    slab, taps, offsets, probe, scan_rows, scan_columns, counts, amplitudes, wf = held
    (
        load, wg, ga, gb,
        bands_f, bands_b, ext, acc, edges, edge_in, img, column_cut, row_cut, column_place, row_place,
        cut, placed,
        a_send, a_recv, h_send, h_recv, e_send, e_recv, b_send, b_recv,
    ) = rest
    loads = [
        pltpu.make_async_copy(inputs[i], held[i], load.at[i]) for i in range(len(inputs))
    ]
    for each in loads:
        each.start()
    rows, width = slab.shape[2], slab.shape[3]
    length = probe.shape[1]
    slots = amplitudes.shape[1]
    tap_count = taps.shape[0]
    size = rows // chunks
    ang = lax.axis_index("ang")
    strip = lax.axis_index("strip")
    has_up = strip > 0
    has_down = strip < strips - 1
    square = n == 4
    if square:
        ax, ay = ang % 2, ang // 2
        near_x, near_y = ay * 2 + (1 - ax), (1 - ay) * 2 + ax
        order = [ang, near_x, near_y, (1 - ay) * 2 + (1 - ax)]
        peers = [near_x, near_y]
    else:
        order = [(ang + n - k) % n for k in range(n)]
        peers = [(ang + k) % n for k in range(1, n)]

    barrier = pltpu.get_barrier_semaphore()
    for peer in peers:
        pl.semaphore_signal(barrier, inc=1, device_id=(peer, strip), device_id_type=MESH)

    @pl.when(has_up)
    def _():
        pl.semaphore_signal(barrier, inc=1, device_id=(ang, strip - 1), device_id_type=MESH)

    @pl.when(has_down)
    def _():
        pl.semaphore_signal(barrier, inc=1, device_id=(ang, strip + 1), device_id_type=MESH)

    sides = (strip + strips - 1) // strips + 1 - (strip + 1) // strips
    pl.semaphore_wait(barrier, len(peers) + sides)

    def part(c):
        return pl.ds(c * size, size)

    def copy(src, dst, send, recv, device):
        return pltpu.make_async_remote_copy(
            src_ref=src, dst_ref=dst, send_sem=send, recv_sem=recv,
            device_id=device, device_id_type=MESH,
        )

    def gather_copy(own, g, send, recv, c, kind):
        if square and kind == 2:
            source, peer = (1, near_y) if c % 2 == 0 else (2, near_x)
            source = g.at[source, :, part(c), :]
        else:
            source, peer = own.at[:, part(c), :], peers[kind]
        return copy(
            source, g.at[kind + 1, :, part(c), :], send.at[kind, c], recv.at[kind, c], (peer, strip)
        )

    def gather_start(own, g, send, recv, c):
        for kind in range(len(peers)):
            gather_copy(own, g, send, recv, c, kind).start()

    def gather_forward(own, g, send, recv, c):
        if square:
            gather_copy(own, g, send, recv, c, c % 2).wait_recv()
            gather_copy(own, g, send, recv, c, 2).start()

    def gather_wait(own, g, send, recv, c):
        for kind in range(n - 1):
            if not (square and kind == c % 2):
                gather_copy(own, g, send, recv, c, kind).wait_recv()

    def gather_sent(own, g, send, recv):
        for c in range(chunks):
            for kind in range(n - 1):
                gather_copy(own, g, send, recv, c, kind).wait_send()

    def strip_copy(src, dst, send, recv, c, way):
        return copy(
            src.at[:, part(c), :], dst.at[way, :, part(c), :], send.at[way, c], recv.at[way, c],
            (ang, strip - 1 if way == 0 else strip + 1),
        )

    def halo_copy(c, way):
        target = 2 * rows if way == 0 else 0
        return copy(
            ext.at[:, pl.ds(rows + c * size, size), :],
            ext.at[:, pl.ds(target + c * size, size), :],
            h_send.at[way, c], h_recv.at[way, c], (ang, strip - 1 if way == 0 else strip + 1),
        )

    def band(k, sign, store):
        if sign > 0:
            angle, depth = ang, order[k]
        else:
            angle, depth = order[k], ang
        offset = offsets[angle, depth]
        weights = [taps[t, angle, depth] for t in range(tap_count)]
        step = 64

        @pl.loop(0, width // step)
        def _(i):
            shape = (step, width)
            source = lax.broadcasted_iota(jnp.int32, shape, 0) + i * step
            target = lax.broadcasted_iota(jnp.int32, shape, 1)
            tap = (source - target) * sign - offset
            value = jnp.zeros(shape, F32)
            for t in range(tap_count):
                value = jnp.where(tap == t, weights[t], value)
            store[k, pl.ds(pl.multiple_of(i * step, step), step), :] = value.astype(BF)

    def apply(own, g, bands, c):
        total = None
        for k in range(n):
            block = own[:, part(c), :] if k == 0 else g[k, :, part(c), :]
            term = jnp.dot(
                block.reshape(2 * size, width), bands[k], preferred_element_type=F32
            )
            total = term if total is None else total + term
        return total.reshape(2, size, width)

    def picks(shape, first, second, shift, live=None):
        hit = (
            lax.broadcasted_iota(jnp.int32, shape, second)
            - lax.broadcasted_iota(jnp.int32, shape, first)
        ) == shift
        if live is not None:
            hit = jnp.logical_and(hit, live)
        return jnp.where(hit, 1.0, 0.0).astype(BF)

    tall = length + rows
    frames = range(slots)
    middle = slice(rows, 2 * rows)
    above, below = slice(0, rows), slice(2 * rows, 3 * rows)

    def dot(left, right):
        return jnp.dot(left, right, preferred_element_type=F32)

    def span(f):
        return slice(f * length, (f + 1) * length)

    def prepare_cuts():
        for f in frames:
            column_cut[:, span(f)] = picks((width, length), 1, 0, scan_columns[0, f])
            row_cut[f] = picks((length, tall), 0, 1, scan_rows[0, f])

    def prepare_places():
        shape = (tall, length)
        for f in frames:
            column_place[f] = picks((length, width), 0, 1, scan_columns[0, f])
            live = lax.broadcasted_iota(jnp.int32, shape, 0) * 0 + f < counts[0, 0]
            row_place[:, span(f)] = picks(shape, 1, 0, scan_rows[0, f], live)
        wg[:length, :] = jnp.concatenate([wf[:length, :length], wf[length:, :length]], axis=1)
        wg[length:, :] = jnp.concatenate([wf[:length, length:], wf[:length, :length]], axis=1)

    def cut_columns(where):
        count = where.stop - where.start
        part_cut = dot(ext[:, where, :].reshape(2 * count, width), column_cut[...]).astype(BF)
        for f in frames:
            cut[f, where, :] = jnp.concatenate(
                [part_cut[:count, span(f)], part_cut[count:, span(f)]], axis=1
            )

    first = slab.at[0]
    loads[0].wait()
    for c in range(min(2, chunks)):
        gather_start(first, ga, a_send, a_recv, c)
    for i in (1, 2):
        loads[i].wait()
    for k in range(n):
        band(k, 1, bands_f)

    def finish(c):
        gather_wait(first, ga, a_send, a_recv, c)
        ext[:, pl.ds(rows + c * size, size), :] = apply(first, ga, bands_f, c).astype(BF)

        @pl.when(has_up)
        def _():
            halo_copy(c, 0).start()

        @pl.when(has_down)
        def _():
            halo_copy(c, 1).start()

    for c in range(chunks):
        gather_forward(first, ga, a_send, a_recv, c)
        if c + 2 < chunks:
            gather_start(first, ga, a_send, a_recv, c + 2)
        if c == 0:
            for each in loads[3:]:
                each.wait()
            prepare_cuts()
        elif c == 1:
            prepare_places()
        if c >= 1:
            finish(c - 1)
    finish(chunks - 1)
    cut_columns(middle)

    @pl.when(has_up)
    def _():
        for c in range(chunks):
            halo_copy(c, 1).wait_recv()

    @pl.when(jnp.logical_not(has_up))
    def _():
        ext[:, :rows, :] = jnp.zeros((2, rows, width), BF)

    @pl.when(has_down)
    def _():
        for c in range(chunks):
            halo_copy(c, 0).wait_recv()

    @pl.when(jnp.logical_not(has_down))
    def _():
        ext[:, 2 * rows :, :] = jnp.zeros((2, rows, width), BF)

    cut_columns(above)
    cut_columns(below)
    probe_real = probe[0].astype(F32)
    probe_imag = probe[1].astype(F32)

    def left(matrix, pair):
        both = dot(matrix[...], jnp.concatenate(pair, axis=0)).astype(BF)
        return jnp.concatenate([both[:length], both[length:]], axis=1)

    waves = []
    for f in frames:
        patch = dot(row_cut[f], cut[f])
        patch_real, patch_imag = patch[:, :length], patch[:, length:]
        waves.append(
            [
                (probe_real * patch_real - probe_imag * patch_imag).astype(BF),
                (probe_real * patch_imag + probe_imag * patch_real).astype(BF),
            ]
        )
    halves = [left(wf, wave) for wave in waves]
    residuals = []
    for f in frames:
        far = dot(halves[f], wg[...])
        far_real, far_imag = far[:, :length], far[:, length:]
        factor = 1.0 - amplitudes[0, f].astype(F32) * lax.rsqrt(
            far_real * far_real + far_imag * far_imag + 1.0
        )
        residuals.append([(far_real * factor).astype(BF), (far_imag * factor).astype(BF)])
    back_halves = [left(wg, residual) for residual in residuals]
    for f in frames:
        back = dot(back_halves[f], wf[...])
        back_real, back_imag = back[:, :length], back[:, length:]
        grad = jnp.concatenate(
            [
                (probe_real * back_real + probe_imag * back_imag).astype(BF),
                (probe_real * back_imag - probe_imag * back_real).astype(BF),
            ],
            axis=0,
        )
        wide = dot(grad, column_place[f]).astype(BF)
        placed[span(f), :] = jnp.concatenate([wide[:length], wide[length:]], axis=1)

    for way, where, here in ((0, above, has_up), (1, below, has_down)):
        edge = dot(row_place[where, :], placed[...]).astype(BF)
        edges[way, 0] = edge[:, :width]
        edges[way, 1] = edge[:, width:]

        @pl.when(here)
        def _(way=way):
            for c in range(chunks):
                strip_copy(edges.at[way], edge_in, e_send, e_recv, c, way).start()

    inner = dot(row_place[middle, :], placed[...])
    acc[0] = inner[:, :width]
    acc[1] = inner[:, width:]
    for k in range(n):
        band(k, -1, bands_b)
    for c in range(chunks):

        @pl.when(has_up)
        def _():
            strip_copy(edges.at[1], edge_in, e_send, e_recv, c, 1).wait_recv()
            acc[:, part(c), :] += edge_in[1, :, part(c), :].astype(F32)

        @pl.when(has_down)
        def _():
            strip_copy(edges.at[0], edge_in, e_send, e_recv, c, 0).wait_recv()
            acc[:, part(c), :] += edge_in[0, :, part(c), :].astype(F32)

        img[:, part(c), :] = acc[:, part(c), :].astype(BF)
        gather_start(img, gb, b_send, b_recv, c)
        if c >= 2:
            gather_forward(img, gb, b_send, b_recv, c - 2)
    for c in range(max(chunks - 2, 0), chunks):
        gather_forward(img, gb, b_send, b_recv, c)
    for c in range(chunks):
        gather_wait(img, gb, b_send, b_recv, c)
        out[0, :, part(c), :] = apply(img, gb, bands_b, c).astype(BF)

    gather_sent(first, ga, a_send, a_recv)
    gather_sent(img, gb, b_send, b_recv)
    for way, here in ((0, has_up), (1, has_down)):

        @pl.when(here)
        def _(way=way):
            for c in range(chunks):
                halo_copy(c, way).wait_send()
                strip_copy(edges.at[way], edge_in, e_send, e_recv, c, way).wait_send()


def per_device(
    n, strips, slab, shear_taps, band_offsets, probe, scan_rows, scan_columns, frame_counts, amplitudes
):
    rows, width = slab.shape[2], slab.shape[3]
    length = probe.shape[1]
    chunks = 4
    slots = amplitudes.shape[1]
    wf = dft_blocks(length)
    small = (1, 2, 4, 5, 6)
    operands = (
        slab, shear_taps, band_offsets, probe, scan_rows, scan_columns, frame_counts, amplitudes,
        jnp.asarray(wf),
    )
    dma = pltpu.SemaphoreType.DMA
    field = (2, rows, width)
    return pl.pallas_call(
        functools.partial(kernel, n, strips, chunks),
        out_shape=jax.ShapeDtypeStruct((1,) + field, BF),
        in_specs=[pl.BlockSpec(memory_space=pltpu.HBM)] * len(operands),
        out_specs=pl.BlockSpec(memory_space=pltpu.VMEM),
        scratch_shapes=[
            (pltpu.SMEM if i in small else pltpu.VMEM)(x.shape, x.dtype)
            for i, x in enumerate(operands)
        ]
        + [
            dma((len(operands),)),
            pltpu.VMEM(wf.shape, BF),
            pltpu.VMEM((n,) + field, BF),
            pltpu.VMEM((n,) + field, BF),
            pltpu.VMEM((n, width, width), BF),
            pltpu.VMEM((n, width, width), BF),
            pltpu.VMEM((2, length + rows, width), BF),
            pltpu.VMEM(field, F32),
            pltpu.VMEM((2,) + field, BF),
            pltpu.VMEM((2,) + field, BF),
            pltpu.VMEM(field, BF),
            pltpu.VMEM((width, slots * length), BF),
            pltpu.VMEM((slots, length, length + rows), BF),
            pltpu.VMEM((slots, length, width), BF),
            pltpu.VMEM((length + rows, slots * length), BF),
            pltpu.VMEM((slots, length + rows, 2 * length), BF),
            pltpu.VMEM((slots * length, 2 * width), BF),
            dma((n - 1, chunks)), dma((n - 1, chunks)),
            dma((2, chunks)), dma((2, chunks)),
            dma((2, chunks)), dma((2, chunks)),
            dma((n - 1, chunks)), dma((n - 1, chunks)),
        ],
        compiler_params=pltpu.CompilerParams(
            collective_id=0, has_side_effects=True, vmem_limit_bytes=62 << 20
        ),
    )(*operands).astype(F32)


def solution(mesh):
    return jax.shard_map(
        functools.partial(per_device, mesh.shape["ang"], mesh.shape["strip"]),
        mesh=mesh,
        in_specs=(
            P("ang", None, "strip", None),
            P(),
            P(),
            P(),
            P("ang", "strip"),
            P("ang", "strip"),
            P("ang", "strip"),
            P("ang", "strip", None, None),
        ),
        out_specs=P("ang", None, "strip", None),
        check_vma=False,
    )
```

```python
import functools
import math

import jax
import jax.numpy as jnp
import ml_dtypes
import numpy as np
from jax import lax
from jax.experimental import pallas as pl
from jax.experimental.pallas import tpu as pltpu
from jax.sharding import PartitionSpec as P

MESH = pl.DeviceIdType.MESH
BF = jnp.bfloat16
F32 = jnp.float32


def dft_blocks(length):
    index = np.arange(length)
    phase = (np.outer(index, index) % length).astype(np.float32) * np.float32(2.0 * math.pi / length)
    scale = np.float32(1.0 / math.sqrt(length))
    cosine = (np.cos(phase) * scale).astype(ml_dtypes.bfloat16)
    sine = (np.sin(phase) * scale).astype(ml_dtypes.bfloat16)
    return np.block([[cosine, sine], [-sine, cosine]])


def kernel(
    n, strips, chunks, *refs,
):
    inputs, out, held, rest = refs[:9], refs[9], refs[10:19], refs[19:]
    slab, taps, offsets, probe, scan_rows, scan_columns, counts, amplitudes, wf = held
    (
        load, wg, ga, gb,
        bands_f, bands_b, ext, acc, edges, edge_in, img, column_cut, row_cut, column_place, row_place,
        cut, placed,
        a_send, a_recv, h_send, h_recv, e_send, e_recv, b_send, b_recv,
    ) = rest
    loads = [
        pltpu.make_async_copy(inputs[i], held[i], load.at[i]) for i in range(len(inputs))
    ]
    for each in loads:
        each.start()
    rows, width = slab.shape[2], slab.shape[3]
    length = probe.shape[1]
    slots = amplitudes.shape[1]
    tap_count = taps.shape[0]
    size = rows // chunks
    ang = lax.axis_index("ang")
    strip = lax.axis_index("strip")
    has_up = strip > 0
    has_down = strip < strips - 1
    square = n == 4
    if square:
        ax, ay = ang % 2, ang // 2
        near_x, near_y = ay * 2 + (1 - ax), (1 - ay) * 2 + ax
        order = [ang, near_x, near_y, (1 - ay) * 2 + (1 - ax)]
        peers = [near_x, near_y]
    else:
        order = [(ang + n - k) % n for k in range(n)]
        peers = [(ang + k) % n for k in range(1, n)]

    barrier = pltpu.get_barrier_semaphore()
    for peer in peers:
        pl.semaphore_signal(barrier, inc=1, device_id=(peer, strip), device_id_type=MESH)

    @pl.when(has_up)
    def _():
        pl.semaphore_signal(barrier, inc=1, device_id=(ang, strip - 1), device_id_type=MESH)

    @pl.when(has_down)
    def _():
        pl.semaphore_signal(barrier, inc=1, device_id=(ang, strip + 1), device_id_type=MESH)

    sides = (strip + strips - 1) // strips + 1 - (strip + 1) // strips
    pl.semaphore_wait(barrier, len(peers) + sides)

    def part(c):
        return pl.ds(c * size, size)

    def copy(src, dst, send, recv, device):
        return pltpu.make_async_remote_copy(
            src_ref=src, dst_ref=dst, send_sem=send, recv_sem=recv,
            device_id=device, device_id_type=MESH,
        )

    def gather_copy(own, g, send, recv, c, kind):
        if square and kind == 2:
            source, peer = (1, near_y) if c % 2 == 0 else (2, near_x)
            source = g.at[source, :, part(c), :]
        else:
            source, peer = own.at[:, part(c), :], peers[kind]
        return copy(
            source, g.at[kind + 1, :, part(c), :], send.at[kind, c], recv.at[kind, c], (peer, strip)
        )

    def gather_start(own, g, send, recv, c):
        for kind in range(len(peers)):
            gather_copy(own, g, send, recv, c, kind).start()

    def gather_forward(own, g, send, recv, c):
        if square:
            gather_copy(own, g, send, recv, c, c % 2).wait_recv()
            gather_copy(own, g, send, recv, c, 2).start()

    def gather_wait(own, g, send, recv, c, kind):
        if not (square and kind == c % 2):
            gather_copy(own, g, send, recv, c, kind).wait_recv()

    def gather_sent(own, g, send, recv):
        for c in range(chunks):
            for kind in range(n - 1):
                gather_copy(own, g, send, recv, c, kind).wait_send()

    def strip_copy(src, dst, send, recv, c, way):
        return copy(
            src.at[:, part(c), :], dst.at[way, :, part(c), :], send.at[way, c], recv.at[way, c],
            (ang, strip - 1 if way == 0 else strip + 1),
        )

    def halo_copy(c, way):
        target = 2 * rows if way == 0 else 0
        return copy(
            ext.at[:, pl.ds(rows + c * size, size), :],
            ext.at[:, pl.ds(target + c * size, size), :],
            h_send.at[way, c], h_recv.at[way, c], (ang, strip - 1 if way == 0 else strip + 1),
        )

    def band(k, sign, store):
        if sign > 0:
            angle, depth = ang, order[k]
        else:
            angle, depth = order[k], ang
        offset = offsets[angle, depth]
        weights = [taps[t, angle, depth] for t in range(tap_count)]
        step = 64

        @pl.loop(0, width // step)
        def _(i):
            shape = (step, width)
            source = lax.broadcasted_iota(jnp.int32, shape, 0) + i * step
            target = lax.broadcasted_iota(jnp.int32, shape, 1)
            tap = (source - target) * sign - offset
            value = jnp.zeros(shape, F32)
            for t in range(tap_count):
                value = jnp.where(tap == t, weights[t], value)
            store[k, pl.ds(pl.multiple_of(i * step, step), step), :] = value.astype(BF)

    def apply(own, g, send, recv, bands, c):
        total = None
        for k in range(n):
            if k > 0:
                gather_wait(own, g, send, recv, c, k - 1)
            block = own[:, part(c), :] if k == 0 else g[k, :, part(c), :]
            term = jnp.dot(
                block.reshape(2 * size, width), bands[k], preferred_element_type=F32
            )
            total = term if total is None else total + term
        return total.reshape(2, size, width)

    def picks(shape, first, second, shift, live=None):
        hit = (
            lax.broadcasted_iota(jnp.int32, shape, second)
            - lax.broadcasted_iota(jnp.int32, shape, first)
        ) == shift
        if live is not None:
            hit = jnp.logical_and(hit, live)
        return jnp.where(hit, 1.0, 0.0).astype(BF)

    tall = length + rows
    frames = range(slots)
    middle = slice(rows, 2 * rows)
    above, below = slice(0, rows), slice(2 * rows, 3 * rows)

    def dot(left, right):
        return jnp.dot(left, right, preferred_element_type=F32)

    def span(f):
        return slice(f * length, (f + 1) * length)

    def prepare_cuts():
        for f in frames:
            column_cut[:, span(f)] = picks((width, length), 1, 0, scan_columns[0, f])
            row_cut[f] = picks((length, tall), 0, 1, scan_rows[0, f])

    def prepare_places():
        shape = (tall, length)
        for f in frames:
            column_place[f] = picks((length, width), 0, 1, scan_columns[0, f])
            live = lax.broadcasted_iota(jnp.int32, shape, 0) * 0 + f < counts[0, 0]
            row_place[:, span(f)] = picks(shape, 1, 0, scan_rows[0, f], live)

    def prepare_transpose():
        wg[:length, :] = jnp.concatenate([wf[:length, :length], wf[length:, :length]], axis=1)
        wg[length:, :] = jnp.concatenate([wf[:length, length:], wf[:length, :length]], axis=1)

    def cut_columns(where):
        count = where.stop - where.start
        part_cut = dot(ext[:, where, :].reshape(2 * count, width), column_cut[...]).astype(BF)
        for f in frames:
            cut[f, where, :] = jnp.concatenate(
                [part_cut[:count, span(f)], part_cut[count:, span(f)]], axis=1
            )

    first = slab.at[0]
    loads[0].wait()
    for c in range(min(3, chunks)):
        gather_start(first, ga, a_send, a_recv, c)
    for i in (1, 2):
        loads[i].wait()
    for k in range(n):
        band(k, 1, bands_f)

    def finish(c):
        piece = apply(first, ga, a_send, a_recv, bands_f, c)
        ext[:, pl.ds(rows + c * size, size), :] = piece.astype(BF)

        @pl.when(has_up)
        def _():
            halo_copy(c, 0).start()

        @pl.when(has_down)
        def _():
            halo_copy(c, 1).start()

    for c in range(chunks):
        gather_forward(first, ga, a_send, a_recv, c)
        if c + 3 < chunks:
            gather_start(first, ga, a_send, a_recv, c + 3)
        if c == 0:
            for each in loads[3:]:
                each.wait()
            prepare_cuts()
        elif c == 1:
            prepare_transpose()
        else:
            finish(c - 2)
    for c in range(max(chunks - 2, 0), chunks):
        finish(c)
    cut_columns(middle)
    prepare_places()

    @pl.when(has_up)
    def _():
        for c in range(chunks):
            halo_copy(c, 1).wait_recv()

    @pl.when(jnp.logical_not(has_up))
    def _():
        ext[:, :rows, :] = jnp.zeros((2, rows, width), BF)

    cut_columns(above)

    @pl.when(has_down)
    def _():
        for c in range(chunks):
            halo_copy(c, 0).wait_recv()

    @pl.when(jnp.logical_not(has_down))
    def _():
        ext[:, 2 * rows :, :] = jnp.zeros((2, rows, width), BF)

    cut_columns(below)
    probe_real = probe[0].astype(F32)
    probe_imag = probe[1].astype(F32)

    def left(matrix, pair):
        both = dot(matrix[...], jnp.concatenate(pair, axis=0)).astype(BF)
        return jnp.concatenate([both[:length], both[length:]], axis=1)

    waves = []
    for f in frames:
        patch = dot(row_cut[f], cut[f])
        patch_real, patch_imag = patch[:, :length], patch[:, length:]
        waves.append(
            [
                (probe_real * patch_real - probe_imag * patch_imag).astype(BF),
                (probe_real * patch_imag + probe_imag * patch_real).astype(BF),
            ]
        )
    halves = [left(wf, wave) for wave in waves]
    residuals = []
    for f in frames:
        far = dot(halves[f], wg[...])
        far_real, far_imag = far[:, :length], far[:, length:]
        factor = 1.0 - amplitudes[0, f].astype(F32) * lax.rsqrt(
            far_real * far_real + far_imag * far_imag + 1.0
        )
        residuals.append([(far_real * factor).astype(BF), (far_imag * factor).astype(BF)])
    back_halves = [left(wg, residual) for residual in residuals]
    for f in frames:
        back = dot(back_halves[f], wf[...])
        back_real, back_imag = back[:, :length], back[:, length:]
        grad = jnp.concatenate(
            [
                (probe_real * back_real + probe_imag * back_imag).astype(BF),
                (probe_real * back_imag - probe_imag * back_real).astype(BF),
            ],
            axis=0,
        )
        wide = dot(grad, column_place[f]).astype(BF)
        placed[span(f), :] = jnp.concatenate([wide[:length], wide[length:]], axis=1)

    for way, where, here in ((0, above, has_up), (1, below, has_down)):
        edge = dot(row_place[where, :], placed[...]).astype(BF)
        edges[way, 0] = edge[:, :width]
        edges[way, 1] = edge[:, width:]

        @pl.when(here)
        def _(way=way):
            for c in range(chunks):
                strip_copy(edges.at[way], edge_in, e_send, e_recv, c, way).start()

    inner = dot(row_place[middle, :], placed[...])
    acc[0] = inner[:, :width]
    acc[1] = inner[:, width:]
    for k in range(n):
        band(k, -1, bands_b)
    for c in range(chunks):

        @pl.when(has_up)
        def _():
            strip_copy(edges.at[1], edge_in, e_send, e_recv, c, 1).wait_recv()
            acc[:, part(c), :] += edge_in[1, :, part(c), :].astype(F32)

        @pl.when(has_down)
        def _():
            strip_copy(edges.at[0], edge_in, e_send, e_recv, c, 0).wait_recv()
            acc[:, part(c), :] += edge_in[0, :, part(c), :].astype(F32)

        img[:, part(c), :] = acc[:, part(c), :].astype(BF)
        gather_start(img, gb, b_send, b_recv, c)
        if c >= 2:
            gather_forward(img, gb, b_send, b_recv, c - 2)
    for c in range(max(chunks - 2, 0), chunks):
        gather_forward(img, gb, b_send, b_recv, c)
    for c in range(chunks):
        out[0, :, part(c), :] = apply(img, gb, b_send, b_recv, bands_b, c)

    gather_sent(first, ga, a_send, a_recv)
    gather_sent(img, gb, b_send, b_recv)
    for way, here in ((0, has_up), (1, has_down)):

        @pl.when(here)
        def _(way=way):
            for c in range(chunks):
                halo_copy(c, way).wait_send()
                strip_copy(edges.at[way], edge_in, e_send, e_recv, c, way).wait_send()


def per_device(
    n, strips, slab, shear_taps, band_offsets, probe, scan_rows, scan_columns, frame_counts, amplitudes
):
    rows, width = slab.shape[2], slab.shape[3]
    length = probe.shape[1]
    chunks = 4
    slots = amplitudes.shape[1]
    wf = dft_blocks(length)
    small = (1, 2, 4, 5, 6)
    operands = (
        slab, shear_taps, band_offsets, probe, scan_rows, scan_columns, frame_counts, amplitudes,
        jnp.asarray(wf),
    )
    dma = pltpu.SemaphoreType.DMA
    field = (2, rows, width)
    return pl.pallas_call(
        functools.partial(kernel, n, strips, chunks),
        out_shape=pltpu.VMEM((1,) + field, F32),
        in_specs=[pl.BlockSpec(memory_space=pltpu.HBM)] * len(operands),
        out_specs=pl.BlockSpec(memory_space=pltpu.VMEM),
        scratch_shapes=[
            (pltpu.SMEM if i in small else pltpu.VMEM)(x.shape, x.dtype)
            for i, x in enumerate(operands)
        ]
        + [
            dma((len(operands),)),
            pltpu.VMEM(wf.shape, BF),
            pltpu.VMEM((n,) + field, BF),
            pltpu.VMEM((n,) + field, BF),
            pltpu.VMEM((n, width, width), BF),
            pltpu.VMEM((n, width, width), BF),
            pltpu.VMEM((2, length + rows, width), BF),
            pltpu.VMEM(field, F32),
            pltpu.VMEM((2,) + field, BF),
            pltpu.VMEM((2,) + field, BF),
            pltpu.VMEM(field, BF),
            pltpu.VMEM((width, slots * length), BF),
            pltpu.VMEM((slots, length, length + rows), BF),
            pltpu.VMEM((slots, length, width), BF),
            pltpu.VMEM((length + rows, slots * length), BF),
            pltpu.VMEM((slots, length + rows, 2 * length), BF),
            pltpu.VMEM((slots * length, 2 * width), BF),
            dma((n - 1, chunks)), dma((n - 1, chunks)),
            dma((2, chunks)), dma((2, chunks)),
            dma((2, chunks)), dma((2, chunks)),
            dma((n - 1, chunks)), dma((n - 1, chunks)),
        ],
        compiler_params=pltpu.CompilerParams(
            collective_id=0, has_side_effects=True, vmem_limit_bytes=62 << 20
        ),
    )(*operands)


def solution(mesh):
    return jax.shard_map(
        functools.partial(per_device, mesh.shape["ang"], mesh.shape["strip"]),
        mesh=mesh,
        in_specs=(
            P("ang", None, "strip", None),
            P(),
            P(),
            P(),
            P("ang", "strip"),
            P("ang", "strip"),
            P("ang", "strip"),
            P("ang", "strip", None, None),
        ),
        out_specs=P("ang", None, "strip", None),
        check_vma=False,
    )
```

```python
import functools
import math

import jax
import jax.numpy as jnp
import ml_dtypes
import numpy as np
from jax import lax
from jax.experimental import pallas as pl
from jax.experimental.pallas import tpu as pltpu
from jax.sharding import PartitionSpec as P

MESH = pl.DeviceIdType.MESH
BF = jnp.bfloat16
F32 = jnp.float32


def dft_blocks(length):
    index = np.arange(length)
    phase = (np.outer(index, index) % length).astype(np.float32) * np.float32(2.0 * math.pi / length)
    scale = np.float32(1.0 / math.sqrt(length))
    cosine = (np.cos(phase) * scale).astype(ml_dtypes.bfloat16)
    sine = (np.sin(phase) * scale).astype(ml_dtypes.bfloat16)
    return np.block([[cosine, sine], [-sine, cosine]])


def kernel(
    n, strips, chunks, *refs,
):
    inputs, out, held, rest = refs[:9], refs[9], refs[10:19], refs[19:]
    slab, taps, offsets, probe, scan_rows, scan_columns, counts, amplitudes, wf = held
    (
        load, wg, ga, gb,
        bands_f, bands_b, ext, acc, edges, edge_in, img, column_cut, row_cut, column_place, row_place,
        cut, placed,
        a_send, a_recv, h_send, h_recv, e_send, e_recv, b_send, b_recv,
    ) = rest
    loads = [
        pltpu.make_async_copy(inputs[i], held[i], load.at[i]) for i in range(len(inputs))
    ]
    for each in loads:
        each.start()
    rows, width = slab.shape[2], slab.shape[3]
    length = probe.shape[1]
    slots = amplitudes.shape[1]
    tap_count = taps.shape[0]
    size = rows // chunks
    ang = lax.axis_index("ang")
    strip = lax.axis_index("strip")
    has_up = strip > 0
    has_down = strip < strips - 1
    square = n == 4
    if square:
        ax, ay = ang % 2, ang // 2
        near_x, near_y = ay * 2 + (1 - ax), (1 - ay) * 2 + ax
        order = [ang, near_x, near_y, (1 - ay) * 2 + (1 - ax)]
        peers = [near_x, near_y]
    else:
        order = [(ang + n - k) % n for k in range(n)]
        peers = [(ang + k) % n for k in range(1, n)]

    barrier = pltpu.get_barrier_semaphore()
    for peer in peers:
        pl.semaphore_signal(barrier, inc=1, device_id=(peer, strip), device_id_type=MESH)

    @pl.when(has_up)
    def _():
        pl.semaphore_signal(barrier, inc=1, device_id=(ang, strip - 1), device_id_type=MESH)

    @pl.when(has_down)
    def _():
        pl.semaphore_signal(barrier, inc=1, device_id=(ang, strip + 1), device_id_type=MESH)

    sides = (strip + strips - 1) // strips + 1 - (strip + 1) // strips
    pl.semaphore_wait(barrier, len(peers) + sides)

    def part(c):
        return pl.ds(c * size, size)

    def copy(src, dst, send, recv, device):
        return pltpu.make_async_remote_copy(
            src_ref=src, dst_ref=dst, send_sem=send, recv_sem=recv,
            device_id=device, device_id_type=MESH,
        )

    def gather_copy(own, g, send, recv, c, kind):
        if square and kind == 2:
            source, peer = (1, near_y) if c % 2 == 0 else (2, near_x)
            source = g.at[source, :, part(c), :]
        else:
            source, peer = own.at[:, part(c), :], peers[kind]
        return copy(
            source, g.at[kind + 1, :, part(c), :], send.at[kind, c], recv.at[kind, c], (peer, strip)
        )

    def gather_start(own, g, send, recv, c):
        for kind in range(len(peers)):
            gather_copy(own, g, send, recv, c, kind).start()

    def gather_forward(own, g, send, recv, c):
        if square:
            gather_copy(own, g, send, recv, c, c % 2).wait_recv()
            gather_copy(own, g, send, recv, c, 2).start()

    def gather_wait(own, g, send, recv, c, kind):
        if not (square and kind == c % 2):
            gather_copy(own, g, send, recv, c, kind).wait_recv()

    def gather_sent(own, g, send, recv):
        for c in range(chunks):
            for kind in range(n - 1):
                gather_copy(own, g, send, recv, c, kind).wait_send()

    def strip_copy(src, dst, send, recv, c, way):
        return copy(
            src.at[:, part(c), :], dst.at[way, :, part(c), :], send.at[way, c], recv.at[way, c],
            (ang, strip - 1 if way == 0 else strip + 1),
        )

    def halo_copy(c, way):
        target = 2 * rows if way == 0 else 0
        return copy(
            ext.at[:, pl.ds(rows + c * size, size), :],
            ext.at[:, pl.ds(target + c * size, size), :],
            h_send.at[way, c], h_recv.at[way, c], (ang, strip - 1 if way == 0 else strip + 1),
        )

    def band(k, sign, store):
        if sign > 0:
            angle, depth = ang, order[k]
        else:
            angle, depth = order[k], ang
        offset = offsets[angle, depth]
        weights = [taps[t, angle, depth] for t in range(tap_count)]
        step = 64

        @pl.loop(0, width // step)
        def _(i):
            shape = (step, width)
            source = lax.broadcasted_iota(jnp.int32, shape, 0) + i * step
            target = lax.broadcasted_iota(jnp.int32, shape, 1)
            tap = (source - target) * sign - offset
            value = jnp.zeros(shape, F32)
            for t in range(tap_count):
                value = jnp.where(tap == t, weights[t], value)
            store[k, pl.ds(pl.multiple_of(i * step, step), step), :] = value.astype(BF)

    def apply(own, g, send, recv, bands, c):
        total = None
        for k in range(n):
            if k > 0:
                gather_wait(own, g, send, recv, c, k - 1)
            block = own[:, part(c), :] if k == 0 else g[k, :, part(c), :]
            term = jnp.dot(
                block.reshape(2 * size, width), bands[k], preferred_element_type=F32
            )
            total = term if total is None else total + term
        return total.reshape(2, size, width)

    def picks(shape, first, second, shift, live=None):
        hit = (
            lax.broadcasted_iota(jnp.int32, shape, second)
            - lax.broadcasted_iota(jnp.int32, shape, first)
        ) == shift
        if live is not None:
            hit = jnp.logical_and(hit, live)
        return jnp.where(hit, 1.0, 0.0).astype(BF)

    tall = length + rows
    frames = range(slots)
    middle = slice(rows, 2 * rows)
    above, below = slice(0, rows), slice(2 * rows, 3 * rows)

    def dot(left, right):
        return jnp.dot(left, right, preferred_element_type=F32)

    def span(f):
        return slice(f * length, (f + 1) * length)

    def prepare_cuts():
        for f in frames:
            column_cut[:, span(f)] = picks((width, length), 1, 0, scan_columns[0, f])
            row_cut[f] = picks((length, tall), 0, 1, scan_rows[0, f])

    def prepare_places():
        shape = (tall, length)
        for f in frames:
            column_place[f] = picks((length, width), 0, 1, scan_columns[0, f])
            live = lax.broadcasted_iota(jnp.int32, shape, 0) * 0 + f < counts[0, 0]
            row_place[:, span(f)] = picks(shape, 1, 0, scan_rows[0, f], live)

    def prepare_transpose():
        wg[:length, :] = jnp.concatenate([wf[:length, :length], wf[length:, :length]], axis=1)
        wg[length:, :] = jnp.concatenate([wf[:length, length:], wf[:length, :length]], axis=1)

    def cut_columns(where):
        count = where.stop - where.start
        part_cut = dot(ext[:, where, :].reshape(2 * count, width), column_cut[...]).astype(BF)
        for f in frames:
            cut[f, where, :] = jnp.concatenate(
                [part_cut[:count, span(f)], part_cut[count:, span(f)]], axis=1
            )

    first = slab.at[0]
    loads[0].wait()
    for c in range(min(3, chunks)):
        gather_start(first, ga, a_send, a_recv, c)
    for i in (1, 2):
        loads[i].wait()
    for k in range(n):
        band(k, 1, bands_f)

    def finish(c):
        piece = apply(first, ga, a_send, a_recv, bands_f, c)
        ext[:, pl.ds(rows + c * size, size), :] = piece.astype(BF)

        @pl.when(has_up)
        def _():
            halo_copy(c, 0).start()

        @pl.when(has_down)
        def _():
            halo_copy(c, 1).start()

    for c in range(chunks):
        gather_forward(first, ga, a_send, a_recv, c)
        if c + 3 < chunks:
            gather_start(first, ga, a_send, a_recv, c + 3)
        if c == 0:
            for each in loads[3:]:
                each.wait()
            prepare_cuts()
        elif c == 1:
            prepare_transpose()
        else:
            finish(c - 2)
    for c in range(max(chunks - 2, 0), chunks):
        finish(c)
    cut_columns(middle)
    prepare_places()

    @pl.when(has_up)
    def _():
        for c in range(chunks):
            halo_copy(c, 1).wait_recv()

    @pl.when(jnp.logical_not(has_up))
    def _():
        ext[:, :rows, :] = jnp.zeros((2, rows, width), BF)

    cut_columns(above)

    @pl.when(has_down)
    def _():
        for c in range(chunks):
            halo_copy(c, 0).wait_recv()

    @pl.when(jnp.logical_not(has_down))
    def _():
        ext[:, 2 * rows :, :] = jnp.zeros((2, rows, width), BF)

    cut_columns(below)
    probe_real = probe[0].astype(F32)
    probe_imag = probe[1].astype(F32)

    def left(matrix, pair):
        both = dot(matrix[...], jnp.concatenate(pair, axis=0)).astype(BF)
        return jnp.concatenate([both[:length], both[length:]], axis=1)

    waves = []
    for f in frames:
        patch = dot(row_cut[f], cut[f])
        patch_real, patch_imag = patch[:, :length], patch[:, length:]
        waves.append(
            [
                (probe_real * patch_real - probe_imag * patch_imag).astype(BF),
                (probe_real * patch_imag + probe_imag * patch_real).astype(BF),
            ]
        )
    halves = [left(wf, wave) for wave in waves]
    residuals = []
    for f in frames:
        far = dot(halves[f], wg[...])
        far_real, far_imag = far[:, :length], far[:, length:]
        factor = 1.0 - amplitudes[0, f].astype(F32) * lax.rsqrt(
            far_real * far_real + far_imag * far_imag + 1.0
        )
        residuals.append([(far_real * factor).astype(BF), (far_imag * factor).astype(BF)])
    back_halves = [left(wg, residual) for residual in residuals]
    for f in frames:
        back = dot(back_halves[f], wf[...])
        back_real, back_imag = back[:, :length], back[:, length:]
        grad = jnp.concatenate(
            [
                (probe_real * back_real + probe_imag * back_imag).astype(BF),
                (probe_real * back_imag - probe_imag * back_real).astype(BF),
            ],
            axis=0,
        )
        wide = dot(grad, column_place[f]).astype(BF)
        placed[span(f), :] = jnp.concatenate([wide[:length], wide[length:]], axis=1)

    for way, where, here in ((0, above, has_up), (1, below, has_down)):
        edge = dot(row_place[where, :], placed[...]).astype(BF)
        edges[way, 0] = edge[:, :width]
        edges[way, 1] = edge[:, width:]

        @pl.when(here)
        def _(way=way):
            for c in range(chunks):
                strip_copy(edges.at[way], edge_in, e_send, e_recv, c, way).start()

    inner = dot(row_place[middle, :], placed[...])
    acc[0] = inner[:, :width]
    acc[1] = inner[:, width:]
    built = 0
    for c in range(chunks):

        @pl.when(has_up)
        def _():
            strip_copy(edges.at[1], edge_in, e_send, e_recv, c, 1).wait_recv()
            acc[:, part(c), :] += edge_in[1, :, part(c), :].astype(F32)

        @pl.when(has_down)
        def _():
            strip_copy(edges.at[0], edge_in, e_send, e_recv, c, 0).wait_recv()
            acc[:, part(c), :] += edge_in[0, :, part(c), :].astype(F32)

        img[:, part(c), :] = acc[:, part(c), :].astype(BF)
        gather_start(img, gb, b_send, b_recv, c)
        if c >= 1:
            band(built, -1, bands_b)
            built += 1
    for c in range(chunks):
        gather_forward(img, gb, b_send, b_recv, c)
        if built < n:
            band(built, -1, bands_b)
            built += 1
    for k in range(built, n):
        band(k, -1, bands_b)
    for c in range(chunks):
        out[0, :, part(c), :] = apply(img, gb, b_send, b_recv, bands_b, c)

    gather_sent(first, ga, a_send, a_recv)
    gather_sent(img, gb, b_send, b_recv)
    for way, here in ((0, has_up), (1, has_down)):

        @pl.when(here)
        def _(way=way):
            for c in range(chunks):
                halo_copy(c, way).wait_send()
                strip_copy(edges.at[way], edge_in, e_send, e_recv, c, way).wait_send()


def per_device(
    n, strips, slab, shear_taps, band_offsets, probe, scan_rows, scan_columns, frame_counts, amplitudes
):
    rows, width = slab.shape[2], slab.shape[3]
    length = probe.shape[1]
    chunks = 4
    slots = amplitudes.shape[1]
    wf = dft_blocks(length)
    small = (1, 2, 4, 5, 6)
    operands = (
        slab, shear_taps, band_offsets, probe, scan_rows, scan_columns, frame_counts, amplitudes,
        jnp.asarray(wf),
    )
    dma = pltpu.SemaphoreType.DMA
    field = (2, rows, width)
    return pl.pallas_call(
        functools.partial(kernel, n, strips, chunks),
        out_shape=pltpu.VMEM((1,) + field, F32),
        in_specs=[pl.BlockSpec(memory_space=pltpu.HBM)] * len(operands),
        out_specs=pl.BlockSpec(memory_space=pltpu.VMEM),
        scratch_shapes=[
            (pltpu.SMEM if i in small else pltpu.VMEM)(x.shape, x.dtype)
            for i, x in enumerate(operands)
        ]
        + [
            dma((len(operands),)),
            pltpu.VMEM(wf.shape, BF),
            pltpu.VMEM((n,) + field, BF),
            pltpu.VMEM((n,) + field, BF),
            pltpu.VMEM((n, width, width), BF),
            pltpu.VMEM((n, width, width), BF),
            pltpu.VMEM((2, length + rows, width), BF),
            pltpu.VMEM(field, F32),
            pltpu.VMEM((2,) + field, BF),
            pltpu.VMEM((2,) + field, BF),
            pltpu.VMEM(field, BF),
            pltpu.VMEM((width, slots * length), BF),
            pltpu.VMEM((slots, length, length + rows), BF),
            pltpu.VMEM((slots, length, width), BF),
            pltpu.VMEM((length + rows, slots * length), BF),
            pltpu.VMEM((slots, length + rows, 2 * length), BF),
            pltpu.VMEM((slots * length, 2 * width), BF),
            dma((n - 1, chunks)), dma((n - 1, chunks)),
            dma((2, chunks)), dma((2, chunks)),
            dma((2, chunks)), dma((2, chunks)),
            dma((n - 1, chunks)), dma((n - 1, chunks)),
        ],
        compiler_params=pltpu.CompilerParams(
            collective_id=0, has_side_effects=True, vmem_limit_bytes=62 << 20
        ),
    )(*operands)


def solution(mesh):
    return jax.shard_map(
        functools.partial(per_device, mesh.shape["ang"], mesh.shape["strip"]),
        mesh=mesh,
        in_specs=(
            P("ang", None, "strip", None),
            P(),
            P(),
            P(),
            P("ang", "strip"),
            P("ang", "strip"),
            P("ang", "strip"),
            P("ang", "strip", None, None),
        ),
        out_specs=P("ang", None, "strip", None),
        check_vma=False,
    )
```

```python
import functools
import math

import jax
import jax.numpy as jnp
import ml_dtypes
import numpy as np
from jax import lax
from jax.experimental import pallas as pl
from jax.experimental.pallas import tpu as pltpu
from jax.sharding import PartitionSpec as P

MESH = pl.DeviceIdType.MESH
BF = jnp.bfloat16
F32 = jnp.float32


def dft_blocks(length):
    index = np.arange(length)
    phase = (np.outer(index, index) % length).astype(np.float32) * np.float32(2.0 * math.pi / length)
    scale = np.float32(1.0 / math.sqrt(length))
    cosine = (np.cos(phase) * scale).astype(ml_dtypes.bfloat16)
    sine = (np.sin(phase) * scale).astype(ml_dtypes.bfloat16)
    return np.block([[cosine, sine], [-sine, cosine]])


def kernel(
    n, strips, chunks, *refs,
):
    inputs, out, held, rest = refs[:9], refs[9], refs[10:19], refs[19:]
    slab, taps, offsets, probe, scan_rows, scan_columns, counts, amplitudes, wf = held
    (
        load, wg, ga, gb,
        bands_f, bands_b, ext, acc, edges, edge_in, img, column_cut, w_rows, probe_rows, column_place, row_place,
        cut, placed,
        a_send, a_recv, h_send, h_recv, e_send, e_recv, b_send, b_recv,
    ) = rest
    loads = [
        pltpu.make_async_copy(inputs[i], held[i], load.at[i]) for i in range(len(inputs))
    ]
    for each in loads:
        each.start()
    rows, width = slab.shape[2], slab.shape[3]
    length = probe.shape[1]
    slots = amplitudes.shape[1]
    tap_count = taps.shape[0]
    size = rows // chunks
    ang = lax.axis_index("ang")
    strip = lax.axis_index("strip")
    has_up = strip > 0
    has_down = strip < strips - 1
    square = n == 4
    if square:
        ax, ay = ang % 2, ang // 2
        near_x, near_y = ay * 2 + (1 - ax), (1 - ay) * 2 + ax
        order = [ang, near_x, near_y, (1 - ay) * 2 + (1 - ax)]
        peers = [near_x, near_y]
    else:
        order = [(ang + n - k) % n for k in range(n)]
        peers = [(ang + k) % n for k in range(1, n)]

    barrier = pltpu.get_barrier_semaphore()
    for peer in peers:
        pl.semaphore_signal(barrier, inc=1, device_id=(peer, strip), device_id_type=MESH)

    @pl.when(has_up)
    def _():
        pl.semaphore_signal(barrier, inc=1, device_id=(ang, strip - 1), device_id_type=MESH)

    @pl.when(has_down)
    def _():
        pl.semaphore_signal(barrier, inc=1, device_id=(ang, strip + 1), device_id_type=MESH)

    sides = (strip + strips - 1) // strips + 1 - (strip + 1) // strips
    pl.semaphore_wait(barrier, len(peers) + sides)

    def part(c):
        return pl.ds(c * size, size)

    def copy(src, dst, send, recv, device):
        return pltpu.make_async_remote_copy(
            src_ref=src, dst_ref=dst, send_sem=send, recv_sem=recv,
            device_id=device, device_id_type=MESH,
        )

    def gather_copy(own, g, send, recv, c, kind):
        if square and kind == 2:
            source, peer = (1, near_y) if c % 2 == 0 else (2, near_x)
            source = g.at[source, :, part(c), :]
        else:
            source, peer = own.at[:, part(c), :], peers[kind]
        return copy(
            source, g.at[kind + 1, :, part(c), :], send.at[kind, c], recv.at[kind, c], (peer, strip)
        )

    def gather_start(own, g, send, recv, c):
        for kind in range(len(peers)):
            gather_copy(own, g, send, recv, c, kind).start()

    def gather_forward(own, g, send, recv, c):
        if square:
            gather_copy(own, g, send, recv, c, c % 2).wait_recv()
            gather_copy(own, g, send, recv, c, 2).start()

    def gather_wait(own, g, send, recv, c, kind):
        if not (square and kind == c % 2):
            gather_copy(own, g, send, recv, c, kind).wait_recv()

    def gather_sent(own, g, send, recv):
        for c in range(chunks):
            for kind in range(n - 1):
                gather_copy(own, g, send, recv, c, kind).wait_send()

    def strip_copy(src, dst, send, recv, c, way):
        return copy(
            src.at[:, part(c), :], dst.at[way, :, part(c), :], send.at[way, c], recv.at[way, c],
            (ang, strip - 1 if way == 0 else strip + 1),
        )

    def halo_copy(c, way):
        target = 2 * rows if way == 0 else 0
        return copy(
            ext.at[:, pl.ds(rows + c * size, size), :],
            ext.at[:, pl.ds(target + c * size, size), :],
            h_send.at[way, c], h_recv.at[way, c], (ang, strip - 1 if way == 0 else strip + 1),
        )

    def band(k, sign, store):
        if sign > 0:
            angle, depth = ang, order[k]
        else:
            angle, depth = order[k], ang
        offset = offsets[angle, depth]
        weights = [taps[t, angle, depth] for t in range(tap_count)]
        step = 64

        @pl.loop(0, width // step)
        def _(i):
            shape = (step, width)
            source = lax.broadcasted_iota(jnp.int32, shape, 0) + i * step
            target = lax.broadcasted_iota(jnp.int32, shape, 1)
            tap = (source - target) * sign - offset
            value = jnp.zeros(shape, F32)
            for t in range(tap_count):
                value = jnp.where(tap == t, weights[t], value)
            store[k, pl.ds(pl.multiple_of(i * step, step), step), :] = value.astype(BF)

    def apply(own, g, send, recv, bands, c):
        total = None
        for k in range(n):
            if k > 0:
                gather_wait(own, g, send, recv, c, k - 1)
            block = own[:, part(c), :] if k == 0 else g[k, :, part(c), :]
            term = jnp.dot(
                block.reshape(2 * size, width), bands[k], preferred_element_type=F32
            )
            total = term if total is None else total + term
        return total.reshape(2, size, width)

    def picks(shape, first, second, shift, live=None):
        hit = (
            lax.broadcasted_iota(jnp.int32, shape, second)
            - lax.broadcasted_iota(jnp.int32, shape, first)
        ) == shift
        if live is not None:
            hit = jnp.logical_and(hit, live)
        return jnp.where(hit, 1.0, 0.0).astype(BF)

    tall = length + rows
    frames = range(slots)
    middle = slice(rows, 2 * rows)
    above, below = slice(0, rows), slice(2 * rows, 3 * rows)

    def dot(left, right):
        return jnp.dot(left, right, preferred_element_type=F32)

    def span(f):
        return slice(f * length, (f + 1) * length)

    def prepare_cuts(some):
        for f in some:
            column_cut[:, span(f)] = picks((width, length), 1, 0, scan_columns[0, f])
            row_cut = picks((length, tall), 0, 1, scan_rows[0, f])
            cosine = dot(wf[:length, :length], row_cut).astype(BF)
            sine = dot(wf[:length, length:], row_cut).astype(BF)
            w_rows[f, :length, :] = jnp.concatenate([cosine, sine], axis=1)
            w_rows[f, length:, :] = jnp.concatenate([-sine, cosine], axis=1)
            probe_rows[f] = dot(
                picks((tall, length), 1, 0, scan_rows[0, f]),
                jnp.concatenate([probe[0], probe[1]], axis=1),
            ).astype(BF)

    def prepare_places():
        shape = (tall, length)
        for f in frames:
            column_place[f] = picks((length, width), 0, 1, scan_columns[0, f])
            live = lax.broadcasted_iota(jnp.int32, shape, 0) * 0 + f < counts[0, 0]
            row_place[:, span(f)] = picks(shape, 1, 0, scan_rows[0, f], live)

    def prepare_transpose():
        wg[:length, :] = jnp.concatenate([wf[:length, :length], wf[length:, :length]], axis=1)
        wg[length:, :] = jnp.concatenate([wf[:length, length:], wf[:length, :length]], axis=1)

    def cut_columns(where):
        count = where.stop - where.start
        part_cut = dot(ext[:, where, :].reshape(2 * count, width), column_cut[...]).astype(BF)
        for f in frames:
            cut[f, where, :] = jnp.concatenate(
                [part_cut[:count, span(f)], part_cut[count:, span(f)]], axis=1
            )

    first = slab.at[0]
    loads[0].wait()
    for c in range(min(3, chunks)):
        gather_start(first, ga, a_send, a_recv, c)
    for i in (1, 2):
        loads[i].wait()
    for k in range(n):
        band(k, 1, bands_f)

    def finish(c):
        piece = apply(first, ga, a_send, a_recv, bands_f, c)
        ext[:, pl.ds(rows + c * size, size), :] = piece.astype(BF)

        @pl.when(has_up)
        def _():
            halo_copy(c, 0).start()

        @pl.when(has_down)
        def _():
            halo_copy(c, 1).start()

    for c in range(chunks):
        gather_forward(first, ga, a_send, a_recv, c)
        if c + 3 < chunks:
            gather_start(first, ga, a_send, a_recv, c + 3)
        if c == 0:
            for each in loads[3:]:
                each.wait()
            prepare_cuts(frames[: slots // 2])
        elif c == 1:
            prepare_cuts(frames[slots // 2 :])
            prepare_transpose()
        else:
            finish(c - 2)
    for c in range(max(chunks - 2, 0), chunks):
        finish(c)
    cut_columns(middle)
    prepare_places()

    @pl.when(has_up)
    def _():
        for c in range(chunks):
            halo_copy(c, 1).wait_recv()

    @pl.when(jnp.logical_not(has_up))
    def _():
        ext[:, :rows, :] = jnp.zeros((2, rows, width), BF)

    cut_columns(above)

    @pl.when(has_down)
    def _():
        for c in range(chunks):
            halo_copy(c, 0).wait_recv()

    @pl.when(jnp.logical_not(has_down))
    def _():
        ext[:, 2 * rows :, :] = jnp.zeros((2, rows, width), BF)

    cut_columns(below)
    probe_real = probe[0].astype(F32)
    probe_imag = probe[1].astype(F32)

    def left(matrix, pair):
        both = dot(matrix[...], jnp.concatenate(pair, axis=0)).astype(BF)
        return jnp.concatenate([both[:length], both[length:]], axis=1)

    waves = []
    for f in frames:
        patch_real = cut[f, :, :length].astype(F32)
        patch_imag = cut[f, :, length:].astype(F32)
        here_real = probe_rows[f, :, :length].astype(F32)
        here_imag = probe_rows[f, :, length:].astype(F32)
        waves.append(
            [
                (here_real * patch_real - here_imag * patch_imag).astype(BF),
                (here_real * patch_imag + here_imag * patch_real).astype(BF),
            ]
        )
    halves = [left(w_rows.at[f], waves[f]) for f in frames]
    residuals = []
    for f in frames:
        far = dot(halves[f], wg[...])
        far_real, far_imag = far[:, :length], far[:, length:]
        factor = 1.0 - amplitudes[0, f].astype(F32) * lax.rsqrt(
            far_real * far_real + far_imag * far_imag + 1.0
        )
        residuals.append([(far_real * factor).astype(BF), (far_imag * factor).astype(BF)])
    back_halves = [left(wg, residual) for residual in residuals]
    for f in frames:
        back = dot(back_halves[f], wf[...])
        back_real, back_imag = back[:, :length], back[:, length:]
        grad = jnp.concatenate(
            [
                (probe_real * back_real + probe_imag * back_imag).astype(BF),
                (probe_real * back_imag - probe_imag * back_real).astype(BF),
            ],
            axis=0,
        )
        wide = dot(grad, column_place[f]).astype(BF)
        placed[span(f), :] = jnp.concatenate([wide[:length], wide[length:]], axis=1)

    for way, where, here in ((0, above, has_up), (1, below, has_down)):
        edge = dot(row_place[where, :], placed[...]).astype(BF)
        edges[way, 0] = edge[:, :width]
        edges[way, 1] = edge[:, width:]

        @pl.when(here)
        def _(way=way):
            for c in range(chunks):
                strip_copy(edges.at[way], edge_in, e_send, e_recv, c, way).start()

    inner = dot(row_place[middle, :], placed[...])
    acc[0] = inner[:, :width]
    acc[1] = inner[:, width:]
    built = 0
    for c in range(chunks):

        @pl.when(has_up)
        def _():
            strip_copy(edges.at[1], edge_in, e_send, e_recv, c, 1).wait_recv()
            acc[:, part(c), :] += edge_in[1, :, part(c), :].astype(F32)

        @pl.when(has_down)
        def _():
            strip_copy(edges.at[0], edge_in, e_send, e_recv, c, 0).wait_recv()
            acc[:, part(c), :] += edge_in[0, :, part(c), :].astype(F32)

        img[:, part(c), :] = acc[:, part(c), :].astype(BF)
        gather_start(img, gb, b_send, b_recv, c)
        if c >= 1:
            band(built, -1, bands_b)
            built += 1
    for c in range(chunks):
        gather_forward(img, gb, b_send, b_recv, c)
        if built < n:
            band(built, -1, bands_b)
            built += 1
    for k in range(built, n):
        band(k, -1, bands_b)
    for c in range(chunks):
        out[0, :, part(c), :] = apply(img, gb, b_send, b_recv, bands_b, c)

    gather_sent(first, ga, a_send, a_recv)
    gather_sent(img, gb, b_send, b_recv)
    for way, here in ((0, has_up), (1, has_down)):

        @pl.when(here)
        def _(way=way):
            for c in range(chunks):
                halo_copy(c, way).wait_send()
                strip_copy(edges.at[way], edge_in, e_send, e_recv, c, way).wait_send()


def per_device(
    n, strips, slab, shear_taps, band_offsets, probe, scan_rows, scan_columns, frame_counts, amplitudes
):
    rows, width = slab.shape[2], slab.shape[3]
    length = probe.shape[1]
    chunks = 4
    slots = amplitudes.shape[1]
    wf = dft_blocks(length)
    small = (1, 2, 4, 5, 6)
    operands = (
        slab, shear_taps, band_offsets, probe, scan_rows, scan_columns, frame_counts, amplitudes,
        jnp.asarray(wf),
    )
    dma = pltpu.SemaphoreType.DMA
    field = (2, rows, width)
    return pl.pallas_call(
        functools.partial(kernel, n, strips, chunks),
        out_shape=pltpu.VMEM((1,) + field, F32),
        in_specs=[pl.BlockSpec(memory_space=pltpu.HBM)] * len(operands),
        out_specs=pl.BlockSpec(memory_space=pltpu.VMEM),
        scratch_shapes=[
            (pltpu.SMEM if i in small else pltpu.VMEM)(x.shape, x.dtype)
            for i, x in enumerate(operands)
        ]
        + [
            dma((len(operands),)),
            pltpu.VMEM(wf.shape, BF),
            pltpu.VMEM((n,) + field, BF),
            pltpu.VMEM((n,) + field, BF),
            pltpu.VMEM((n, width, width), BF),
            pltpu.VMEM((n, width, width), BF),
            pltpu.VMEM((2, length + rows, width), BF),
            pltpu.VMEM(field, F32),
            pltpu.VMEM((2,) + field, BF),
            pltpu.VMEM((2,) + field, BF),
            pltpu.VMEM(field, BF),
            pltpu.VMEM((width, slots * length), BF),
            pltpu.VMEM((slots, 2 * length, 2 * (length + rows)), BF),
            pltpu.VMEM((slots, length + rows, 2 * length), BF),
            pltpu.VMEM((slots, length, width), BF),
            pltpu.VMEM((length + rows, slots * length), BF),
            pltpu.VMEM((slots, length + rows, 2 * length), BF),
            pltpu.VMEM((slots * length, 2 * width), BF),
            dma((n - 1, chunks)), dma((n - 1, chunks)),
            dma((2, chunks)), dma((2, chunks)),
            dma((2, chunks)), dma((2, chunks)),
            dma((n - 1, chunks)), dma((n - 1, chunks)),
        ],
        compiler_params=pltpu.CompilerParams(
            collective_id=0, has_side_effects=True, vmem_limit_bytes=62 << 20
        ),
    )(*operands)


def solution(mesh):
    return jax.shard_map(
        functools.partial(per_device, mesh.shape["ang"], mesh.shape["strip"]),
        mesh=mesh,
        in_specs=(
            P("ang", None, "strip", None),
            P(),
            P(),
            P(),
            P("ang", "strip"),
            P("ang", "strip"),
            P("ang", "strip"),
            P("ang", "strip", None, None),
        ),
        out_specs=P("ang", None, "strip", None),
        check_vma=False,
    )
```
